32 devices in a mesh: groups: 2 (over y), tp: 4 (over z), dp: 2 (over x), sub: 2 (over core).
Axes of the slice: x: 2, y: 2, z: 4, core: 2. Of those that a mesh axis runs over, the one named last changes fastest.
Arguments:
- queries: bfloat16 [32, 8192], P(('groups', 'dp', 'sub'), 'tp'), parts along dimension 0, may hold values from -8 to 8
- key_value_cache: bfloat16 [32, 2, 512, 1024], P(('groups', 'dp', 'sub'), None, 'tp'), parts along dimension 0, may hold values from -8 to 8
- fresh_token_entries: bfloat16 [32, 2, 1024], P(('groups', 'dp', 'sub')), parts along dimension 0, may hold values from -6 to 6
- lengths: int32 [32], P(('groups', 'dp', 'sub')), parts along dimension 0, may hold values from 128 to 512, as said below
- frozen_base_matrix: bfloat16 [8192, 5120], P('tp'), may hold values from -0.0625 to 0.0625
- lowrank_down_factor: bfloat16 [32, 8192], P('groups', ('tp', 'sub')), parts along dimension 0, may hold values from -0.375 to 0.375
- lowrank_up_factor: bfloat16 [32, 5120], P('groups', ('tp', 'sub')), parts along dimension 0, may hold values from -0.09375 to 0.09375
- magnitude: bfloat16 [10240], P(('groups', 'tp', 'sub')), parts along dimension 0, may hold values from 2 to 20
- piece_owner_blocks: int32 [16], P('groups'), parts along dimension 0, may hold values from 0 to 7, each once
Outputs:
- projected: bfloat16 [32, 5120], P(('groups', 'dp', 'sub'), 'tp'), parts along dimension 0
The draws below stay inside these ranges and needn't reach their ends.
There are 2 independent parts, one for each index of `groups`. The reference program is written for one: setup_inputs(seed, part) draws one part's arguments, and reference() takes and returns one part's arrays. A program takes and returns all parts, laid end to end along the dimension named above; an argument that names none is the same for every part. Nothing has to cross between parts.
Inputs may be any that keep to these rules, and one draw needn't show every extreme that they name: piece_owner_blocks is a permutation. `lengths`: some sequence has all 512 positions cached.
All inputs are finite; a program needn't handle non-finite values.
Results may differ from the reference program's by a relative error of at most 0.0063.
Values may be sent and summed in bfloat16 or wider, within the bound.
A program may use at most 192 MiB of HBM per device.

```python
import math
import jax
import jax.numpy as jnp
from jax import lax

MODEL_WIDTH = 5120
HEADS = 64
KVH = 8
HD = 128
UPDATE_RANK = 16
PROJECT_INPUTS = 8192
BATCH = 16
CTX = 512
TRAINER_PIECES = 8


def draw_queries(key, part):
    key = jax.random.fold_in(key, 5)
    values = jnp.clip(jax.random.normal(key, (BATCH, HEADS, HD), jnp.float32), -6.0, 6.0)
    return values.reshape(BATCH, HEADS * HD).astype(jnp.bfloat16)


def draw_key_value_cache(key, part):
    key = jax.random.fold_in(key, 7)
    values = jnp.clip(jax.random.normal(key, (BATCH, 2, CTX, KVH * HD), jnp.float32), -6.0, 6.0)
    return values.astype(jnp.bfloat16)


def draw_lengths(key, part):
    key = jax.random.fold_in(key, 9)
    counts = jax.random.randint(key, (BATCH,), CTX // 4, CTX + 1)
    chosen_row = jax.random.randint(jax.random.fold_in(key, 1), (), 0, BATCH)
    return jnp.where(jnp.arange(BATCH) == chosen_row, CTX, counts).astype(jnp.int32)


def block_scale(key, dims, split, low, high):
    def one(dim, blocks):
        steps = jax.random.uniform(jax.random.fold_in(jax.random.fold_in(key, 6), dim), (blocks,), jnp.float32, low / len(split), high / len(split))
        return jnp.repeat(jnp.exp(steps), dims[dim] // blocks).reshape((-1,) + (1,) * (len(dims) - dim - 1))

    loudness = one(*split[0])
    for cut in split[1:]:
        loudness = loudness * one(*cut)
    return loudness


def centred(stream_key, shape, scale, bound, pieces=(), kind=jnp.bfloat16):
    level = block_scale(stream_key, shape, pieces, -0.22, 0.18) if pieces else 1.0
    result = jax.random.normal(stream_key, shape, jnp.float32) * scale * level
    return jnp.minimum(jnp.maximum(result, -bound), bound).astype(kind)


def setup_inputs(seed: int = 0, part: int = 0) -> dict:
    seeds = jax.random.split(jax.random.key(seed), 10)
    part_splits = jax.random.split(jax.random.fold_in(seeds[9], part), 10)
    queries = draw_queries(jax.random.fold_in(jax.random.fold_in(seeds[9], part), 71), part)
    key_value_cache = draw_key_value_cache(jax.random.fold_in(jax.random.fold_in(seeds[9], part), 71), part)
    fresh_token_entries = centred(part_splits[2], (BATCH, 2, KVH * HD), 1.0, 6.0, ((0, 4),))
    lengths = draw_lengths(jax.random.fold_in(jax.random.fold_in(seeds[9], part), 71), part)
    frozen_base_matrix = centred(seeds[4], (PROJECT_INPUTS, MODEL_WIDTH), PROJECT_INPUTS ** -0.5, 0.0625, ((0, 4),))
    lowrank_down_factor = centred(part_splits[5], (UPDATE_RANK, PROJECT_INPUTS), 256 ** -0.5, 0.375, ((1, 8),))
    lowrank_up_factor = centred(part_splits[6], (UPDATE_RANK, MODEL_WIDTH), 4096 ** -0.5, 0.09375, ((1, 8),))
    magnitude = jnp.clip(jnp.exp(math.log(20.0) - 2.3025851 * jax.random.uniform(part_splits[7], (MODEL_WIDTH,), jnp.float32) ** block_scale(part_splits[7], (MODEL_WIDTH,), ((0, 8),), -0.2, 0.2)), 2.0, 20.0).astype(jnp.bfloat16)
    piece_owner_blocks = jax.random.permutation(part_splits[8], TRAINER_PIECES).astype(jnp.int32)
    return dict(queries=queries, key_value_cache=key_value_cache, fresh_token_entries=fresh_token_entries, lengths=lengths, frozen_base_matrix=frozen_base_matrix, lowrank_down_factor=lowrank_down_factor, lowrank_up_factor=lowrank_up_factor, magnitude=magnitude, piece_owner_blocks=piece_owner_blocks)


norm_eps = 1e-06

def arrange_down_factor(lowrank_down_factor, piece_owner_blocks):
    rollout_block_rows = HEADS * HD // TRAINER_PIECES
    trainer_parts = lowrank_down_factor.reshape(UPDATE_RANK, TRAINER_PIECES, rollout_block_rows)
    placed = jnp.zeros_like(trainer_parts).at[:, piece_owner_blocks, :].set(trainer_parts)
    return placed.reshape(UPDATE_RANK, HEADS * HD)

def merge_output_weight(frozen_base_matrix, rollout_down_factor, lowrank_up_factor, magnitude):
    lowrank_update = lax.dot_general(rollout_down_factor, lowrank_up_factor, (((0,), (0,)), ((), ())), preferred_element_type=jnp.float32)
    combined = frozen_base_matrix.astype(jnp.float32) + lowrank_update
    column_norms = jnp.sqrt(lax.optimization_barrier(jnp.sum(combined * combined, axis=0)) + norm_eps)
    return (combined * (magnitude.astype(jnp.float32) / column_norms)).astype(jnp.bfloat16)

def attend_one(inputs):
    query_row, cache_row, entry_row, length_row = inputs
    group_size = HEADS // KVH
    score_scale = HD ** (-0.5)
    query_heads = query_row.reshape(KVH, group_size, HD).astype(jnp.float32)
    keys = cache_row[0].reshape(CTX, KVH, HD).astype(jnp.float32)
    values = cache_row[1].reshape(CTX, KVH, HD).astype(jnp.float32)
    new_key = entry_row[0].reshape(KVH, HD).astype(jnp.float32)
    new_value = entry_row[1].reshape(KVH, HD).astype(jnp.float32)
    scores = jnp.einsum('kgd,pkd->kgp', query_heads, keys) * score_scale
    own_score = jnp.einsum('kgd,kd->kg', query_heads, new_key) * score_scale
    valid_mask = jnp.arange(CTX) < length_row
    scores = jnp.where(valid_mask, scores, -1e+30)
    peak_all = jnp.maximum(lax.optimization_barrier(jnp.max(scores, axis=-1)), own_score)
    weights = jnp.where(valid_mask, jnp.exp(scores - peak_all[..., None]), 0.0)
    own_weight = jnp.exp(own_score - peak_all)
    rounded = lax.optimization_barrier(weights.astype(jnp.bfloat16)).astype(jnp.float32)
    own_rounded = lax.optimization_barrier(own_weight.astype(jnp.bfloat16)).astype(jnp.float32)
    numer = jnp.einsum('kgp,pkd->kgd', rounded, values) + own_rounded[..., None] * new_value[:, None, :]
    denom = lax.optimization_barrier(jnp.sum(weights, axis=-1)) + own_weight
    return (numer / denom[..., None]).reshape(HEADS * HD).astype(jnp.bfloat16)

def reference(queries, key_value_cache, fresh_token_entries, lengths, frozen_base_matrix, lowrank_down_factor, lowrank_up_factor, magnitude, piece_owner_blocks):
    rollout_down_factor = arrange_down_factor(lowrank_down_factor, piece_owner_blocks)
    merged_matrix = merge_output_weight(frozen_base_matrix, rollout_down_factor, lowrank_up_factor, magnitude)
    context = lax.map(attend_one, (queries, key_value_cache, fresh_token_entries, lengths))
    return jnp.dot(context, merged_matrix, preferred_element_type=jnp.float32).astype(jnp.bfloat16)
```

```python
import functools

import jax
import jax.numpy as jnp
from jax import lax
from jax.experimental import pallas as pl
from jax.experimental.pallas import tpu as pltpu
from jax.sharding import PartitionSpec as P

HEADS = 64
KVH = 8
HD = 128
UPDATE_RANK = 16


norm_eps = 1e-06


def expand_rank(down_cols, up_rows):
    return lax.dot_general(
        down_cols, up_rows, (((0,), (0,)), ((), ())), preferred_element_type=jnp.float32
    )


def local(
    queries,
    key_value_cache,
    fresh_token_entries,
    lengths,
    frozen_base_matrix,
    lowrank_down_factor,
    lowrank_up_factor,
    magnitude,
    piece_owner_blocks,
):
    local_rows = frozen_base_matrix.shape[0]
    seq_count = queries.shape[0]
    cache_len = key_value_cache.shape[2]
    group_size = HEADS // KVH
    score_scale = HD ** (-0.5)
    tp_index = lax.axis_index("tp")
    down_all, up_all, magnitudes = (
        lax.all_gather(lowrank_down_factor, ("tp", "sub"), axis=1, tiled=True),
        lax.all_gather(lowrank_up_factor, ("tp", "sub"), axis=1, tiled=True),
        lax.all_gather(magnitude, ("tp", "sub"), axis=0, tiled=True),
    )
    piece_count = piece_owner_blocks.shape[0]
    rollout_block_rows = down_all.shape[1] // piece_count
    blocks_own = local_rows // rollout_block_rows
    wanted = tp_index * blocks_own + jnp.arange(blocks_own)
    selector = (piece_owner_blocks[None, :] == wanted[:, None]).astype(jnp.bfloat16)
    down_local = (
        jnp.einsum(
            "jk,rkc->rjc",
            selector,
            down_all.reshape(UPDATE_RANK, piece_count, rollout_block_rows),
            preferred_element_type=jnp.float32,
        )
        .astype(jnp.bfloat16)
        .reshape(UPDATE_RANK, local_rows)
    )
    query_all = lax.all_gather(queries, "tp", axis=1, tiled=True).reshape(
        seq_count, KVH, group_size, HD
    )
    keys_local = key_value_cache[:, 0].reshape(seq_count, cache_len, KVH, HD)
    values_local = key_value_cache[:, 1].reshape(seq_count, cache_len, KVH, HD)
    positions = tp_index * cache_len + jnp.arange(cache_len)
    valid_mask = positions[None, :] < lengths[:, None]
    scores = (
        jnp.einsum("skgd,spkd->skgp", query_all, keys_local, preferred_element_type=jnp.float32)
        * score_scale
    )
    scores = jnp.where(valid_mask[:, None, None, :], scores, -1e30)
    peak_part = lax.pmax(jnp.max(scores, axis=-1), "tp")
    new_key = fresh_token_entries[:, 0].reshape(seq_count, KVH, HD)
    new_value = fresh_token_entries[:, 1].reshape(seq_count, KVH, HD).astype(jnp.float32)
    own_score = (
        jnp.einsum("skgd,skd->skg", query_all, new_key, preferred_element_type=jnp.float32)
        * score_scale
    )
    peak_all = jnp.maximum(peak_part, own_score)
    weights = jnp.where(valid_mask[:, None, None, :], jnp.exp(scores - peak_all[..., None]), 0.0)
    weighted = jnp.einsum(
        "skgp,spkd->skgd",
        weights.astype(jnp.bfloat16),
        values_local,
        preferred_element_type=jnp.float32,
    )
    weights_sum = jnp.sum(weights, axis=-1)
    combined = frozen_base_matrix.astype(jnp.float32) + expand_rank(down_local, up_all)
    square_part = jnp.sum(combined * combined, axis=0)
    own_weight = jnp.exp(own_score - peak_all)
    own_rounded = lax.optimization_barrier(own_weight.astype(jnp.bfloat16)).astype(jnp.float32)
    column_total = lax.psum(square_part, "tp")
    weighted_all, weights_all = lax.psum((weighted, weights_sum), "tp")
    numer = weighted_all + own_rounded[..., None] * new_value[:, :, None, :]
    denom = weights_all + own_weight
    context = (numer / denom[..., None]).reshape(seq_count, HEADS * HD).astype(jnp.bfloat16)
    context_local = lax.dynamic_slice_in_dim(context, tp_index * local_rows, local_rows, 1)
    column_norms = jnp.sqrt(column_total + norm_eps)
    merged_matrix = (combined * (magnitudes.astype(jnp.float32) / column_norms)).astype(
        jnp.bfloat16
    )
    partial_out = jnp.dot(context_local, merged_matrix, preferred_element_type=jnp.float32)
    return lax.psum_scatter(partial_out, "tp", scatter_dimension=1, tiled=True).astype(jnp.bfloat16)


def fused_kernel(
    sizes,
    lengths_ref,
    owner_ref,
    query_ref,
    fresh_ref,
    down_ref,
    up_ref,
    magnitude_ref,
    cache_ref,
    base_ref,
    out_ref,
    query_f32,
    query_all,
    cache,
    base,
    combined,
    pieces,
    down_local,
    up,
    magnitudes,
    part_send,
    part_recv,
    context_all,
    context_f32,
    norm_acc,
    norm_send,
    norm_recv,
    proj_send,
    proj_recv,
    cache_sem,
    base_sem,
    query_s,
    query_r,
    piece_s,
    piece_r,
    forward_s,
    forward_r,
    up_s,
    up_r,
    mag_s,
    mag_r,
    part_s,
    part_r,
    context_s,
    context_r,
    norm_s,
    norm_r,
    proj_s,
    proj_r,
):
    tp, dp, sub = sizes["tp"], sizes["dp"], sizes["sub"]
    owners = dp * sub
    t, d, s = lax.axis_index("tp"), lax.axis_index("dp"), lax.axis_index("sub")
    q = d * sub + s
    other = 1 - s
    seqs = query_ref.shape[0]
    heads = HEADS // tp
    half = heads // 2
    rows, columns = base.shape
    cache_len = cache.shape[2]
    score_scale = HD ** (-0.5)
    f32, bf16 = jnp.float32, jnp.bfloat16

    def place(tp_index, owner):
        return {"tp": tp_index, "dp": owner // sub, "sub": lax.rem(owner, sub)}

    def remote(src, dst, send, recv, where):
        return pltpu.make_async_remote_copy(
            src_ref=src,
            dst_ref=dst,
            send_sem=send,
            recv_sem=recv,
            device_id=where,
            device_id_type=pl.DeviceIdType.MESH,
        )

    cache_copies = [
        pltpu.make_async_copy(cache_ref.at[:, i], cache.at[:, i], cache_sem.at[i]) for i in range(2)
    ]
    for copy in cache_copies:
        copy.start()
    base_copy = pltpu.make_async_copy(
        base_ref.at[:, pl.ds(pl.multiple_of(q * columns, columns), columns)], base, base_sem
    )
    base_copy.start()

    barrier = pltpu.get_barrier_semaphore()
    for r in range(tp):
        for k in range(owners):
            if r or k:
                pl.semaphore_signal(
                    barrier,
                    inc=1,
                    device_id=place(lax.rem(t + r, tp), lax.rem(q + k, owners)),
                    device_id_type=pl.DeviceIdType.MESH,
                )

    for h in range(heads):
        query_f32[pl.ds(h, seqs, stride=heads), :] = query_ref[:, h * HD : (h + 1) * HD].astype(f32)
    own_query = query_f32[...].reshape(seqs, heads, HD)
    query_all[t] = own_query.astype(bf16)
    pieces[t * sub + s] = down_ref[...]
    magnitudes[s] = magnitude_ref[...].astype(f32)

    pl.semaphore_wait(barrier, tp * owners - 1)

    query_copies, piece_copies = [], []
    for r in range(1, tp):
        peer = lax.rem(t + r, tp)
        copy = remote(
            query_all.at[t], query_all.at[t], query_s.at[r], query_r.at[t], place(peer, q)
        )
        copy.start()
        query_copies.append(copy)
    mag_copy = remote(
        magnitudes.at[s], magnitudes.at[s], mag_s, mag_r, place(t, d * sub + other)
    )
    for r in range(1, tp):
        peer = lax.rem(t + r, tp)
        mine = t * sub + s
        copy = remote(pieces.at[mine], pieces.at[mine], piece_s.at[r], piece_r.at[t], place(peer, q))
        copy.start()
        piece_copies.append(copy)

    def forward(tp_index):
        which = tp_index * sub + s
        return remote(
            pieces.at[which],
            pieces.at[which],
            forward_s.at[tp_index],
            forward_r.at[tp_index],
            place(t, d * sub + other),
        )

    forward(t).start()
    mag_copy.start()

    up_here = d == t // sub
    up_owner = lax.rem(t, sub)

    def up_copy(r):
        return remote(
            up_ref, up.at[s], up_s.at[r], up_r.at[s], place(lax.rem(t + r, tp), t)
        )

    up_self = jnp.logical_and(up_here, s == up_owner)

    @pl.when(up_here)
    def _():
        for r in range(1, tp):
            up_copy(r).start()

    @pl.when(jnp.logical_and(up_here, s != up_owner))
    def _():
        up_copy(0).start()

    @pl.when(up_self)
    def _():
        up[s] = up_ref[...]

    row_index = lax.broadcasted_iota(jnp.int32, (heads, HD), 0)
    lane_index = lax.broadcasted_iota(jnp.int32, (heads, HD), 1)
    upper = row_index < half
    position = t * cache_len + lax.broadcasted_iota(jnp.int32, (heads, cache_len), 1)

    for copy in cache_copies:
        copy.wait()

    def attend(tp_index):
        span = pl.ds(pl.multiple_of(tp_index * 2 * HD, 2 * HD), 2 * HD)
        stats = jnp.zeros((heads, HD), f32)
        for i in range(seqs):
            query = query_all[tp_index, i].astype(f32)
            left = jnp.where(upper, query, 0.0).astype(bf16)
            right = jnp.where(upper, 0.0, query).astype(bf16)
            scores = (
                lax.dot_general(
                    jnp.concatenate([left, right], axis=1),
                    cache[i, 0, :, span],
                    (((1,), (1,)), ((), ())),
                    preferred_element_type=f32,
                )
                * score_scale
            )
            valid = position < lengths_ref[i]
            scores = jnp.where(valid, scores, -1e30)
            peak = jnp.max(scores, axis=-1, keepdims=True)
            weights = jnp.where(valid, jnp.exp(scores - peak), 0.0)
            total = jnp.sum(weights, axis=-1, keepdims=True)
            both = jnp.dot(
                weights.astype(bf16), cache[i, 1, :, span], preferred_element_type=f32
            )
            part_send[tp_index, i] = jnp.where(upper, both[:, :HD], both[:, HD:])
            stats = jnp.where(lane_index == i, peak, stats)
            stats = jnp.where(lane_index == seqs + i, total, stats)
        part_send[tp_index, seqs] = stats

    attend(t)
    part_recv[t] = part_send[t]
    part_copies = []
    for r in range(1, tp):
        peer = lax.rem(t + tp - r, tp)
        remote(
            query_all.at[peer], query_all.at[peer], query_s.at[r], query_r.at[peer], place(peer, q)
        ).wait_recv()
        attend(peer)
        copy = remote(
            part_send.at[peer], part_recv.at[t], part_s.at[r], part_r.at[t], place(peer, q)
        )
        copy.start()
        part_copies.append(copy)

    for r in range(1, tp):
        peer = lax.rem(t + tp - r, tp)
        which = peer * sub + s
        remote(
            pieces.at[which], pieces.at[which], piece_s.at[r], piece_r.at[peer], place(peer, q)
        ).wait_recv()
        forward(peer).start()

    for j in range(sub):

        @pl.when(jnp.logical_or(t != q, s != j))
        def _():
            remote(up_ref, up.at[j], up_s.at[0], up_r.at[j], place(t, q)).wait_recv()

    for r in range(tp):
        peer = lax.rem(t + r, tp)
        which = peer * sub + other
        remote(
            pieces.at[which],
            pieces.at[which],
            forward_s.at[peer],
            forward_r.at[peer],
            place(t, d * sub + other),
        ).wait_recv()

    piece_rows = pieces.shape[2]
    for j in range(rows // piece_rows):
        wanted = t * (rows // piece_rows) + j
        found = jnp.int32(0)
        for k in range(pieces.shape[0]):
            found = jnp.where(owner_ref[k] == wanted, k, found)
        down_local[:, j * piece_rows : (j + 1) * piece_rows] = pieces[found]

    base_copy.wait()
    norm_acc[...] = jnp.zeros_like(norm_acc)
    block = 256
    up_all = jnp.concatenate([up[j] for j in range(sub)], axis=1)

    def merge(c, carry):
        here = pl.ds(pl.multiple_of(c * block, block), block)
        down_rows = down_local[:, here]
        for n in range(columns // block):
            cols = slice(n * block, (n + 1) * block)
            tile = base[here, cols].astype(f32) + lax.dot_general(
                down_rows, up_all[:, cols], (((0,), (0,)), ((), ())), preferred_element_type=f32
            )
            norm_acc[:, cols] += jnp.sum((tile * tile).reshape(block // 8, 8, block), axis=0)
            combined[here, cols] = tile.astype(bf16)
        return carry

    lax.fori_loop(0, rows // block, merge, 0)
    norm_send[...] = jnp.sum(norm_acc[...], axis=0, keepdims=True)

    def result_copy(src, dst, send, recv, k):
        return remote(
            src, dst.at[t], send.at[k], recv.at[t], place(q, lax.rem(q + k, owners))
        )

    itself = t == q

    def norm_copy(k):
        return result_copy(norm_send, norm_recv, norm_s, norm_r, k)

    for k in range(1, owners):
        norm_copy(k).start()

    @pl.when(jnp.logical_not(itself))
    def _():
        norm_copy(0).start()

    @pl.when(itself)
    def _():
        norm_recv[t] = norm_send[...]

    fresh = [
        [
            fresh_ref[
                i, :, pl.ds(pl.multiple_of((t * 2 + j) * HD, HD), HD)
            ].astype(f32)
            for j in range(2)
        ]
        for i in range(seqs)
    ]
    own_scores, own_values = [], []
    for i in range(seqs):
        key = jnp.where(upper, fresh[i][0][0:1], fresh[i][1][0:1])
        own_values.append(jnp.where(upper, fresh[i][0][1:2], fresh[i][1][1:2]))
        rows_of_query = query_f32[i * heads : (i + 1) * heads, :]
        own_scores.append(jnp.sum(rows_of_query * key, axis=-1, keepdims=True) * score_scale)

    for r in range(1, tp):
        peer = lax.rem(t + r, tp)
        remote(
            part_send.at[peer], part_recv.at[peer], part_s.at[r], part_r.at[peer], place(peer, q)
        ).wait_recv()

    all_stats = [part_recv[k, seqs] for k in range(tp)]
    for i in range(seqs):
        peaks = [x[:, i : i + 1] for x in all_stats]
        peak = own_scores[i]
        for x in peaks:
            peak = jnp.maximum(peak, x)
        own_weight = jnp.exp(own_scores[i] - peak)
        numer = own_weight.astype(bf16).astype(f32) * own_values[i]
        denom = own_weight
        for k in range(tp):
            factor = jnp.exp(peaks[k] - peak)
            numer = numer + factor * part_recv[k, i]
            denom = denom + factor * all_stats[k][:, seqs + i : seqs + i + 1]
        context_all[q, i] = (numer / denom).astype(bf16)

    context_copies = []
    for k in range(1, owners):
        copy = remote(
            context_all.at[q],
            context_all.at[q],
            context_s.at[k],
            context_r.at[q],
            place(t, lax.rem(q + k, owners)),
        )
        copy.start()
        context_copies.append(copy)
    for k in range(1, owners):
        peer = lax.rem(q + k, owners)
        remote(
            context_all.at[peer],
            context_all.at[peer],
            context_s.at[k],
            context_r.at[peer],
            place(t, peer),
        ).wait_recv()

    total_seqs = owners * seqs
    context_f32[...] = context_all[...].astype(f32).reshape(total_seqs * heads, HD)
    context = jnp.concatenate(
        [context_f32[pl.ds(h, total_seqs, stride=heads), :].astype(bf16) for h in range(heads)],
        axis=1,
    )
    middle = columns // 2
    for n in range(columns // block):
        partial = jnp.dot(
            context, combined[:, n * block : (n + 1) * block], preferred_element_type=f32
        )
        for piece in range(block // HD):
            start = n * block + piece * HD
            side, lane = start // middle, start % middle
            for k in range(owners):
                proj_send[k, side * seqs : (side + 1) * seqs, lane : lane + HD] = partial[
                    k * seqs : (k + 1) * seqs, piece * HD : (piece + 1) * HD
                ]

    def proj_copy(k):
        return result_copy(
            proj_send.at[lax.rem(q + k, owners)], proj_recv, proj_s, proj_r, k
        )

    for k in range(1, owners):
        proj_copy(k).start()

    @pl.when(jnp.logical_not(itself))
    def _():
        proj_copy(0).start()

    @pl.when(itself)
    def _():
        proj_recv[t] = proj_send[q]

    remote(
        magnitudes.at[other], magnitudes.at[other], mag_s, mag_r, place(t, d * sub + other)
    ).wait_recv()

    def arrived(src, dst, send, recv):
        for k in range(tp):

            @pl.when(jnp.logical_or(q != t, t != k))
            def _():
                remote(src, dst.at[k], send.at[0], recv.at[k], place(k, t)).wait_recv()

    arrived(norm_send, norm_recv, norm_s, norm_r)
    squares = norm_recv[0]
    for k in range(1, tp):
        squares = squares + norm_recv[k]
    norms = jnp.sqrt(squares + norm_eps)
    arrived(proj_send.at[0], proj_recv, proj_s, proj_r)
    total = proj_recv[0]
    for k in range(1, tp):
        total = total + proj_recv[k]
    for side in range(2):
        scale = magnitudes[side] / norms[:, side * middle : (side + 1) * middle]
        out_ref[:, side * middle : (side + 1) * middle] = (
            total[side * seqs : (side + 1) * seqs] * scale
        ).astype(bf16)

    for copy in query_copies + piece_copies + part_copies + context_copies:
        copy.wait_send()
    mag_copy.wait_send()
    for r in range(tp):
        forward(lax.rem(t + r, tp)).wait_send()

    @pl.when(up_here)
    def _():
        for r in range(1, tp):
            up_copy(r).wait_send()

    @pl.when(jnp.logical_and(up_here, s != up_owner))
    def _():
        up_copy(0).wait_send()

    for k in range(1, owners):
        norm_copy(k).wait_send()
        proj_copy(k).wait_send()

    @pl.when(jnp.logical_not(itself))
    def _():
        norm_copy(0).wait_send()
        proj_copy(0).wait_send()


def fused_local(
    sizes,
    queries,
    key_value_cache,
    fresh_token_entries,
    lengths,
    frozen_base_matrix,
    lowrank_down_factor,
    lowrank_up_factor,
    magnitude,
    piece_owner_blocks,
):
    tp, dp, sub = sizes["tp"], sizes["dp"], sizes["sub"]
    owners = dp * sub
    seqs = queries.shape[0]
    heads = HEADS // tp
    rows, width = frozen_base_matrix.shape
    columns = width // owners
    trainers = tp * sub
    f32, bf16 = jnp.float32, jnp.bfloat16
    sem = pltpu.SemaphoreType.DMA
    vmem = pl.BlockSpec(memory_space=pltpu.VMEM)
    smem = pl.BlockSpec(memory_space=pltpu.SMEM)
    anywhere = pl.BlockSpec(memory_space=pl.ANY)
    return pl.pallas_call(
        functools.partial(fused_kernel, sizes),
        out_shape=jax.ShapeDtypeStruct((seqs, width // tp), bf16),
        in_specs=[smem, smem, vmem, vmem, vmem, vmem, vmem, anywhere, anywhere],
        out_specs=vmem,
        scratch_shapes=[
            pltpu.VMEM((seqs * heads, HD), f32),
            pltpu.VMEM((tp, seqs, heads, HD), bf16),
            pltpu.VMEM(key_value_cache.shape, bf16),
            pltpu.VMEM((rows, columns), bf16),
            pltpu.VMEM((rows, columns), bf16),
            pltpu.VMEM((trainers,) + lowrank_down_factor.shape, bf16),
            pltpu.VMEM((UPDATE_RANK, rows), bf16),
            pltpu.VMEM((sub,) + lowrank_up_factor.shape, bf16),
            pltpu.VMEM((sub, 1, magnitude.shape[0]), f32),
            pltpu.VMEM((tp, seqs + 1, heads, HD), f32),
            pltpu.VMEM((tp, seqs + 1, heads, HD), f32),
            pltpu.VMEM((owners, seqs, heads, HD), bf16),
            pltpu.VMEM((owners * seqs * heads, HD), f32),
            pltpu.VMEM((8, columns), f32),
            pltpu.VMEM((1, columns), f32),
            pltpu.VMEM((tp, 1, columns), f32),
            pltpu.VMEM((owners, 2 * seqs, columns // 2), f32),
            pltpu.VMEM((tp, 2 * seqs, columns // 2), f32),
            sem((2,)),
            sem,
            sem((tp,)),
            sem((tp,)),
            sem((tp,)),
            sem((tp,)),
            sem((tp,)),
            sem((tp,)),
            sem((tp,)),
            sem((sub,)),
            sem,
            sem,
            sem((tp,)),
            sem((tp,)),
            sem((owners,)),
            sem((owners,)),
            sem((owners,)),
            sem((tp,)),
            sem((owners,)),
            sem((tp,)),
        ],
        compiler_params=pltpu.CompilerParams(
            collective_id=0, has_side_effects=True, vmem_limit_bytes=56 * 1024 * 1024
        ),
    )(
        lengths,
        piece_owner_blocks,
        queries,
        fresh_token_entries,
        lowrank_down_factor,
        lowrank_up_factor,
        magnitude.reshape(1, -1),
        key_value_cache,
        frozen_base_matrix,
    )


def solution(mesh):
    in_specs = (
        P(("groups", "dp", "sub"), "tp"),
        P(("groups", "dp", "sub"), None, "tp", None),
        P(("groups", "dp", "sub"), None, None),
        P(("groups", "dp", "sub")),
        P("tp", None),
        P("groups", ("tp", "sub")),
        P("groups", ("tp", "sub")),
        P(("groups", "tp", "sub")),
        P("groups"),
    )
    out_specs = P(("groups", "dp", "sub"), "tp")
    sizes = dict(mesh.shape)
    owners = sizes["dp"] * sizes["sub"]
    fits = sizes["tp"] == owners and 2 * sizes["tp"] == KVH and sizes["sub"] == 2
    body = functools.partial(fused_local, sizes) if fits else local
    return jax.shard_map(body, mesh=mesh, in_specs=in_specs, out_specs=out_specs, check_vma=False)
```

```python
import functools

import jax
import jax.numpy as jnp
from jax import lax
from jax.experimental import pallas as pl
from jax.experimental.pallas import tpu as pltpu
from jax.sharding import PartitionSpec as P

HEADS = 64
KVH = 8
HD = 128
UPDATE_RANK = 16


norm_eps = 1e-06


def expand_rank(down_cols, up_rows):
    return lax.dot_general(
        down_cols, up_rows, (((0,), (0,)), ((), ())), preferred_element_type=jnp.float32
    )


def local(
    queries,
    key_value_cache,
    fresh_token_entries,
    lengths,
    frozen_base_matrix,
    lowrank_down_factor,
    lowrank_up_factor,
    magnitude,
    piece_owner_blocks,
):
    local_rows = frozen_base_matrix.shape[0]
    seq_count = queries.shape[0]
    cache_len = key_value_cache.shape[2]
    group_size = HEADS // KVH
    score_scale = HD ** (-0.5)
    tp_index = lax.axis_index("tp")
    down_all, up_all, magnitudes = (
        lax.all_gather(lowrank_down_factor, ("tp", "sub"), axis=1, tiled=True),
        lax.all_gather(lowrank_up_factor, ("tp", "sub"), axis=1, tiled=True),
        lax.all_gather(magnitude, ("tp", "sub"), axis=0, tiled=True),
    )
    piece_count = piece_owner_blocks.shape[0]
    rollout_block_rows = down_all.shape[1] // piece_count
    blocks_own = local_rows // rollout_block_rows
    wanted = tp_index * blocks_own + jnp.arange(blocks_own)
    selector = (piece_owner_blocks[None, :] == wanted[:, None]).astype(jnp.bfloat16)
    down_local = (
        jnp.einsum(
            "jk,rkc->rjc",
            selector,
            down_all.reshape(UPDATE_RANK, piece_count, rollout_block_rows),
            preferred_element_type=jnp.float32,
        )
        .astype(jnp.bfloat16)
        .reshape(UPDATE_RANK, local_rows)
    )
    query_all = lax.all_gather(queries, "tp", axis=1, tiled=True).reshape(
        seq_count, KVH, group_size, HD
    )
    keys_local = key_value_cache[:, 0].reshape(seq_count, cache_len, KVH, HD)
    values_local = key_value_cache[:, 1].reshape(seq_count, cache_len, KVH, HD)
    positions = tp_index * cache_len + jnp.arange(cache_len)
    valid_mask = positions[None, :] < lengths[:, None]
    scores = (
        jnp.einsum("skgd,spkd->skgp", query_all, keys_local, preferred_element_type=jnp.float32)
        * score_scale
    )
    scores = jnp.where(valid_mask[:, None, None, :], scores, -1e30)
    peak_part = lax.pmax(jnp.max(scores, axis=-1), "tp")
    new_key = fresh_token_entries[:, 0].reshape(seq_count, KVH, HD)
    new_value = fresh_token_entries[:, 1].reshape(seq_count, KVH, HD).astype(jnp.float32)
    own_score = (
        jnp.einsum("skgd,skd->skg", query_all, new_key, preferred_element_type=jnp.float32)
        * score_scale
    )
    peak_all = jnp.maximum(peak_part, own_score)
    weights = jnp.where(valid_mask[:, None, None, :], jnp.exp(scores - peak_all[..., None]), 0.0)
    weighted = jnp.einsum(
        "skgp,spkd->skgd",
        weights.astype(jnp.bfloat16),
        values_local,
        preferred_element_type=jnp.float32,
    )
    weights_sum = jnp.sum(weights, axis=-1)
    combined = frozen_base_matrix.astype(jnp.float32) + expand_rank(down_local, up_all)
    square_part = jnp.sum(combined * combined, axis=0)
    own_weight = jnp.exp(own_score - peak_all)
    own_rounded = lax.optimization_barrier(own_weight.astype(jnp.bfloat16)).astype(jnp.float32)
    column_total = lax.psum(square_part, "tp")
    weighted_all, weights_all = lax.psum((weighted, weights_sum), "tp")
    numer = weighted_all + own_rounded[..., None] * new_value[:, :, None, :]
    denom = weights_all + own_weight
    context = (numer / denom[..., None]).reshape(seq_count, HEADS * HD).astype(jnp.bfloat16)
    context_local = lax.dynamic_slice_in_dim(context, tp_index * local_rows, local_rows, 1)
    column_norms = jnp.sqrt(column_total + norm_eps)
    merged_matrix = (combined * (magnitudes.astype(jnp.float32) / column_norms)).astype(
        jnp.bfloat16
    )
    partial_out = jnp.dot(context_local, merged_matrix, preferred_element_type=jnp.float32)
    return lax.psum_scatter(partial_out, "tp", scatter_dimension=1, tiled=True).astype(jnp.bfloat16)


def fused_kernel(
    sizes,
    lengths_ref,
    owner_ref,
    query_ref,
    fresh_ref,
    down_ref,
    up_ref,
    magnitude_ref,
    cache_ref,
    base_ref,
    out_ref,
    query_f32,
    query_all,
    cache,
    base,
    combined,
    pieces,
    down_local,
    up,
    magnitudes,
    part_send,
    part_recv,
    context_all,
    context_f32,
    norm_acc,
    norm_send,
    norm_recv,
    proj_send,
    proj_recv,
    cache_sem,
    base_sem,
    query_s,
    query_r,
    piece_s,
    piece_r,
    forward_s,
    forward_r,
    up_s,
    up_r,
    own_s,
    own_r,
    mag_s,
    mag_r,
    part_s,
    part_r,
    context_s,
    context_r,
    norm_s,
    norm_r,
    proj_s,
    proj_r,
):
    tp, dp, sub = sizes["tp"], sizes["dp"], sizes["sub"]
    owners = dp * sub
    t, d, s = lax.axis_index("tp"), lax.axis_index("dp"), lax.axis_index("sub")
    q = d + dp * s
    other = 1 - s
    seqs = query_ref.shape[0]
    heads = HEADS // tp
    half = heads // 2
    rows, columns = base.shape
    cache_len = cache.shape[2]
    score_scale = HD ** (-0.5)
    f32, bf16 = jnp.float32, jnp.bfloat16

    def place(tp_index, owner):
        return {"tp": tp_index, "dp": lax.rem(owner, dp), "sub": owner // dp}

    def peer_of(r):
        if r == 1:
            return t + 1 - 2 * lax.rem(t, 2)
        if r == 2:
            return t + 2 - 4 * (t // 2)
        return tp - 1 - t

    def remote(src, dst, send, recv, where):
        return pltpu.make_async_remote_copy(
            src_ref=src,
            dst_ref=dst,
            send_sem=send,
            recv_sem=recv,
            device_id=where,
            device_id_type=pl.DeviceIdType.MESH,
        )

    cache_copies = [
        pltpu.make_async_copy(cache_ref.at[:, i], cache.at[:, i], cache_sem.at[i]) for i in range(2)
    ]
    for copy in cache_copies:
        copy.start()
    base_copy = pltpu.make_async_copy(
        base_ref.at[:, pl.ds(pl.multiple_of(q * columns, columns), columns)], base, base_sem
    )
    base_copy.start()

    barrier = pltpu.get_barrier_semaphore()
    greeted = [place(peer_of(r), q) for r in range(1, tp)]
    greeted += [place(t, lax.rem(q + k, owners)) for k in range(1, owners)]
    for where in greeted:
        pl.semaphore_signal(
            barrier, inc=1, device_id=where, device_id_type=pl.DeviceIdType.MESH
        )

    for h in range(heads):
        query_f32[pl.ds(h, seqs, stride=heads), :] = query_ref[:, h * HD : (h + 1) * HD].astype(f32)
    own_query = query_f32[...].reshape(seqs, heads, HD)
    query_all[t] = own_query.astype(bf16)
    pieces[t * sub + s] = down_ref[...]
    magnitudes[s] = magnitude_ref[...].astype(f32).reshape(1, -1)

    row_index = lax.broadcasted_iota(jnp.int32, (heads, HD), 0)
    lane_index = lax.broadcasted_iota(jnp.int32, (heads, HD), 1)
    upper = row_index < half
    position = t * cache_len + lax.broadcasted_iota(jnp.int32, (heads, cache_len), 1)

    for copy in cache_copies:
        copy.wait()

    def split3(value):
        terms = []
        for _ in range(3):
            term = value.astype(bf16).astype(f32)
            terms.append(term)
            value = value - term
        return terms

    def joined(stats, first, i):
        lanes = [stats[:, (first + n) * seqs + i : (first + n) * seqs + i + 1] for n in range(3)]
        return (lanes[0] + lanes[1]) + lanes[2]

    def attend(tp_index):
        span = pl.ds(pl.multiple_of(tp_index * 2 * HD, 2 * HD), 2 * HD)
        stats = jnp.zeros((heads, HD), f32)
        for i in range(seqs):
            query = query_all[tp_index, i].astype(f32)
            left = jnp.where(upper, query, 0.0).astype(bf16)
            right = jnp.where(upper, 0.0, query).astype(bf16)
            scores = (
                lax.dot_general(
                    jnp.concatenate([left, right], axis=1),
                    cache[i, 0, :, span],
                    (((1,), (1,)), ((), ())),
                    preferred_element_type=f32,
                )
                * score_scale
            )
            valid = position < lengths_ref[i]
            scores = jnp.where(valid, scores, -1e30)
            peak = jnp.max(scores, axis=-1, keepdims=True)
            weights = jnp.where(valid, jnp.exp(scores - peak), 0.0)
            total = jnp.sum(weights, axis=-1, keepdims=True)
            both = jnp.dot(
                weights.astype(bf16), cache[i, 1, :, span], preferred_element_type=f32
            )
            part_send[tp_index, i] = jnp.where(upper, both[:, :HD], both[:, HD:]).astype(bf16)
            for term, value in enumerate(split3(peak) + split3(total)):
                stats = jnp.where(lane_index == term * seqs + i, value, stats)
        part_send[tp_index, seqs] = stats.astype(bf16)

    attend(t)
    part_recv[t] = part_send[t]

    pl.semaphore_wait(barrier, len(greeted))

    sibling = place(t, d + dp * other)
    mine = t * sub + s
    piece_columns = pieces.shape[2] // dp

    def part_of(piece, which_half):
        return pieces.at[
            piece, :, pl.ds(pl.multiple_of(which_half * piece_columns, piece_columns), piece_columns)
        ]

    query_copies, piece_copies = [], []
    for r in (3, 2, 1):
        copy = remote(
            query_all.at[t], query_all.at[t], query_s.at[r], query_r.at[t], place(peer_of(r), q)
        )
        copy.start()
        query_copies.append(copy)
    for r in (3, 2, 1):
        copy = remote(
            part_of(mine, d),
            part_of(mine, d),
            piece_s.at[r],
            piece_r.at[t],
            place(peer_of(r), q),
        )
        copy.start()
        piece_copies.append(copy)
    for src, send, recv in ((pieces.at[mine], own_s, own_r), (magnitudes.at[s], mag_s, mag_r)):
        copy = remote(src, src, send, recv, sibling)
        copy.start()
        piece_copies.append(copy)

    up_here = d == lax.rem(t, dp)
    up_owner = t // dp

    def up_copy(r):
        return remote(
            up_ref, up.at[s], up_s.at[r], up_r.at[s], place(peer_of(r) if r else t, t)
        )

    up_self = jnp.logical_and(up_here, s == up_owner)

    @pl.when(jnp.logical_and(up_here, s != up_owner))
    def _():
        up_copy(0).start()

    @pl.when(up_self)
    def _():
        up[s] = up_ref[...]

    part_copies = []
    for r in range(1, tp):
        peer = peer_of(r)
        remote(
            query_all.at[peer], query_all.at[peer], query_s.at[r], query_r.at[peer], place(peer, q)
        ).wait_recv()
        attend(peer)

        @pl.when(up_here)
        def _():
            up_copy(r).start()

        copy = remote(
            part_send.at[peer], part_recv.at[t], part_s.at[r], part_r.at[t], place(peer, q)
        )
        copy.start()
        part_copies.append(copy)

    forward_copies = []
    for r in range(1, tp):
        peer = peer_of(r)
        got = part_of(peer * sub + s, d)
        remote(got, got, piece_s.at[r], piece_r.at[peer], place(peer, q)).wait_recv()
        for k in range(1, owners):
            copy = remote(
                got,
                got,
                forward_s.at[r, k],
                forward_r.at[peer, q],
                place(t, lax.rem(q + k, owners)),
            )
            copy.start()
            forward_copies.append(copy)

    for j in range(sub):

        @pl.when(jnp.logical_or(t != q, s != j))
        def _():
            remote(up_ref, up.at[j], up_s.at[0], up_r.at[j], place(t, q)).wait_recv()

    got = pieces.at[t * sub + other]
    remote(got, got, own_s, own_r, sibling).wait_recv()
    for r in range(1, tp):
        peer = peer_of(r)
        for k in range(1, owners):
            source = lax.rem(q + k, owners)
            got = part_of(peer * sub + source // dp, lax.rem(source, dp))
            remote(
                got, got, forward_s.at[r, k], forward_r.at[peer, source], place(t, source)
            ).wait_recv()

    piece_rows = pieces.shape[2]
    for j in range(rows // piece_rows):
        wanted = t * (rows // piece_rows) + j
        found = jnp.int32(0)
        for k in range(pieces.shape[0]):
            found = jnp.where(owner_ref[k] == wanted, k, found)
        down_local[:, j * piece_rows : (j + 1) * piece_rows] = pieces[found]

    base_copy.wait()
    norm_acc[...] = jnp.zeros_like(norm_acc)
    block = 256
    up_all = jnp.concatenate([up[j] for j in range(sub)], axis=1)

    def merge(c, carry):
        here = pl.ds(pl.multiple_of(c * block, block), block)
        down_rows = down_local[:, here]
        for n in range(columns // block):
            cols = slice(n * block, (n + 1) * block)
            tile = base[here, cols].astype(f32) + lax.dot_general(
                down_rows, up_all[:, cols], (((0,), (0,)), ((), ())), preferred_element_type=f32
            )
            norm_acc[:, cols] += jnp.sum((tile * tile).reshape(block // 8, 8, block), axis=0)
            combined[here, cols] = tile.astype(bf16)
        return carry

    lax.fori_loop(0, rows // block, merge, 0)
    norm_send[...] = jnp.sum(norm_acc[...], axis=0, keepdims=True)

    def result_copy(src, dst, send, recv, k):
        return remote(
            src, dst.at[t], send.at[k], recv.at[t], place(q, lax.rem(q + k, owners))
        )

    itself = t == q

    def norm_copy(k):
        return result_copy(norm_send, norm_recv, norm_s, norm_r, k)

    for k in range(1, owners):
        norm_copy(k).start()

    @pl.when(jnp.logical_not(itself))
    def _():
        norm_copy(0).start()

    @pl.when(itself)
    def _():
        norm_recv[t] = norm_send[...]

    fresh = [
        [
            fresh_ref[
                i, :, pl.ds(pl.multiple_of((t * 2 + j) * HD, HD), HD)
            ].astype(f32)
            for j in range(2)
        ]
        for i in range(seqs)
    ]
    own_scores, own_values = [], []
    for i in range(seqs):
        key = jnp.where(upper, fresh[i][0][0:1], fresh[i][1][0:1])
        own_values.append(jnp.where(upper, fresh[i][0][1:2], fresh[i][1][1:2]))
        rows_of_query = query_f32[i * heads : (i + 1) * heads, :]
        own_scores.append(jnp.sum(rows_of_query * key, axis=-1, keepdims=True) * score_scale)

    for r in range(1, tp):
        peer = peer_of(r)
        remote(
            part_send.at[peer], part_recv.at[peer], part_s.at[r], part_r.at[peer], place(peer, q)
        ).wait_recv()

    all_stats = [part_recv[k, seqs].astype(f32) for k in range(tp)]
    for i in range(seqs):
        peaks = [joined(x, 0, i) for x in all_stats]
        peak = own_scores[i]
        for x in peaks:
            peak = jnp.maximum(peak, x)
        own_weight = jnp.exp(own_scores[i] - peak)
        numer = own_weight.astype(bf16).astype(f32) * own_values[i]
        denom = own_weight
        for k in range(tp):
            factor = jnp.exp(peaks[k] - peak)
            numer = numer + factor * part_recv[k, i].astype(f32)
            denom = denom + factor * joined(all_stats[k], 3, i)
        context_all[q, i] = (numer / denom).astype(bf16)

    context_copies = []
    for k in range(1, owners):
        copy = remote(
            context_all.at[q],
            context_all.at[q],
            context_s.at[k],
            context_r.at[q],
            place(t, lax.rem(q + k, owners)),
        )
        copy.start()
        context_copies.append(copy)
    for k in range(1, owners):
        peer = lax.rem(q + k, owners)
        remote(
            context_all.at[peer],
            context_all.at[peer],
            context_s.at[k],
            context_r.at[peer],
            place(t, peer),
        ).wait_recv()

    total_seqs = owners * seqs
    context_f32[...] = context_all[...].astype(f32).reshape(total_seqs * heads, HD)
    context = jnp.concatenate(
        [context_f32[pl.ds(h, total_seqs, stride=heads), :].astype(bf16) for h in range(heads)],
        axis=1,
    )
    middle = columns // 2
    for n in range(columns // block):
        partial = jnp.dot(
            context, combined[:, n * block : (n + 1) * block], preferred_element_type=f32
        )
        for piece in range(block // HD):
            start = n * block + piece * HD
            side, lane = start // middle, start % middle
            for k in range(owners):
                proj_send[k, side * seqs : (side + 1) * seqs, lane : lane + HD] = partial[
                    k * seqs : (k + 1) * seqs, piece * HD : (piece + 1) * HD
                ]

    def proj_copy(k):
        return result_copy(
            proj_send.at[lax.rem(q + k, owners)], proj_recv, proj_s, proj_r, k
        )

    for k in range(1, owners):
        proj_copy(k).start()

    @pl.when(jnp.logical_not(itself))
    def _():
        proj_copy(0).start()

    @pl.when(itself)
    def _():
        proj_recv[t] = proj_send[q]

    remote(
        magnitudes.at[other], magnitudes.at[other], mag_s, mag_r, sibling
    ).wait_recv()

    def arrived(src, dst, send, recv):
        for k in range(tp):

            @pl.when(jnp.logical_or(q != t, t != k))
            def _():
                remote(src, dst.at[k], send.at[0], recv.at[k], place(k, t)).wait_recv()

    arrived(norm_send, norm_recv, norm_s, norm_r)
    squares = norm_recv[0]
    for k in range(1, tp):
        squares = squares + norm_recv[k]
    norms = jnp.sqrt(squares + norm_eps)
    arrived(proj_send.at[0], proj_recv, proj_s, proj_r)
    total = proj_recv[0]
    for k in range(1, tp):
        total = total + proj_recv[k]
    for side in range(2):
        scale = magnitudes[side] / norms[:, side * middle : (side + 1) * middle]
        out_ref[:, side * middle : (side + 1) * middle] = (
            total[side * seqs : (side + 1) * seqs] * scale
        ).astype(bf16)

    for copy in query_copies + piece_copies + forward_copies + part_copies + context_copies:
        copy.wait_send()

    @pl.when(up_here)
    def _():
        for r in range(1, tp):
            up_copy(r).wait_send()

    @pl.when(jnp.logical_and(up_here, s != up_owner))
    def _():
        up_copy(0).wait_send()

    for k in range(1, owners):
        norm_copy(k).wait_send()
        proj_copy(k).wait_send()

    @pl.when(jnp.logical_not(itself))
    def _():
        norm_copy(0).wait_send()
        proj_copy(0).wait_send()


def fused_local(
    sizes,
    queries,
    key_value_cache,
    fresh_token_entries,
    lengths,
    frozen_base_matrix,
    lowrank_down_factor,
    lowrank_up_factor,
    magnitude,
    piece_owner_blocks,
):
    tp, dp, sub = sizes["tp"], sizes["dp"], sizes["sub"]
    owners = dp * sub
    seqs = queries.shape[0]
    heads = HEADS // tp
    rows, width = frozen_base_matrix.shape
    columns = width // owners
    trainers = tp * sub
    f32, bf16 = jnp.float32, jnp.bfloat16
    sem = pltpu.SemaphoreType.DMA
    vmem = pl.BlockSpec(memory_space=pltpu.VMEM)
    smem = pl.BlockSpec(memory_space=pltpu.SMEM)
    anywhere = pl.BlockSpec(memory_space=pl.ANY)
    return pl.pallas_call(
        functools.partial(fused_kernel, sizes),
        out_shape=jax.ShapeDtypeStruct((seqs, width // tp), bf16),
        in_specs=[smem, smem, vmem, vmem, vmem, vmem, vmem, anywhere, anywhere],
        out_specs=vmem,
        scratch_shapes=[
            pltpu.VMEM((seqs * heads, HD), f32),
            pltpu.VMEM((tp, seqs, heads, HD), bf16),
            pltpu.VMEM(key_value_cache.shape, bf16),
            pltpu.VMEM((rows, columns), bf16),
            pltpu.VMEM((rows, columns), bf16),
            pltpu.VMEM((trainers,) + lowrank_down_factor.shape, bf16),
            pltpu.VMEM((UPDATE_RANK, rows), bf16),
            pltpu.VMEM((sub,) + lowrank_up_factor.shape, bf16),
            pltpu.VMEM((sub, 1, magnitude.shape[0]), f32),
            pltpu.VMEM((tp, seqs + 1, heads, HD), bf16),
            pltpu.VMEM((tp, seqs + 1, heads, HD), bf16),
            pltpu.VMEM((owners, seqs, heads, HD), bf16),
            pltpu.VMEM((owners * seqs * heads, HD), f32),
            pltpu.VMEM((8, columns), f32),
            pltpu.VMEM((1, columns), f32),
            pltpu.VMEM((tp, 1, columns), f32),
            pltpu.VMEM((owners, 2 * seqs, columns // 2), f32),
            pltpu.VMEM((tp, 2 * seqs, columns // 2), f32),
            sem((2,)),
            sem,
            sem((tp,)),
            sem((tp,)),
            sem((tp,)),
            sem((tp,)),
            sem((tp, owners)),
            sem((tp, owners)),
            sem((tp,)),
            sem((sub,)),
            sem,
            sem,
            sem,
            sem,
            sem((tp,)),
            sem((tp,)),
            sem((owners,)),
            sem((owners,)),
            sem((owners,)),
            sem((tp,)),
            sem((owners,)),
            sem((tp,)),
        ],
        compiler_params=pltpu.CompilerParams(
            collective_id=0, has_side_effects=True, vmem_limit_bytes=56 * 1024 * 1024
        ),
    )(
        lengths,
        piece_owner_blocks,
        queries,
        fresh_token_entries,
        lowrank_down_factor,
        lowrank_up_factor,
        magnitude,
        key_value_cache,
        frozen_base_matrix,
    )


def solution(mesh):
    in_specs = (
        P(("groups", "dp", "sub"), "tp"),
        P(("groups", "dp", "sub"), None, "tp", None),
        P(("groups", "dp", "sub"), None, None),
        P(("groups", "dp", "sub")),
        P("tp", None),
        P("groups", ("tp", "sub")),
        P("groups", ("tp", "sub")),
        P(("groups", "tp", "sub")),
        P("groups"),
    )
    out_specs = P(("groups", "dp", "sub"), "tp")
    sizes = dict(mesh.shape)
    owners = sizes["dp"] * sizes["sub"]
    fits = sizes["tp"] == owners and 2 * sizes["tp"] == KVH and sizes["sub"] == 2
    body = functools.partial(fused_local, sizes) if fits else local
    return jax.shard_map(body, mesh=mesh, in_specs=in_specs, out_specs=out_specs, check_vma=False)
```

```python
import functools

import jax
import jax.numpy as jnp
from jax import lax
from jax.experimental import pallas as pl
from jax.experimental.pallas import tpu as pltpu
from jax.sharding import PartitionSpec as P

HEADS = 64
KVH = 8
HD = 128
UPDATE_RANK = 16


norm_eps = 1e-06


def expand_rank(down_cols, up_rows):
    return lax.dot_general(
        down_cols, up_rows, (((0,), (0,)), ((), ())), preferred_element_type=jnp.float32
    )


def local(
    queries,
    key_value_cache,
    fresh_token_entries,
    lengths,
    frozen_base_matrix,
    lowrank_down_factor,
    lowrank_up_factor,
    magnitude,
    piece_owner_blocks,
):
    local_rows = frozen_base_matrix.shape[0]
    seq_count = queries.shape[0]
    cache_len = key_value_cache.shape[2]
    group_size = HEADS // KVH
    score_scale = HD ** (-0.5)
    tp_index = lax.axis_index("tp")
    down_all, up_all, magnitudes = (
        lax.all_gather(lowrank_down_factor, ("tp", "sub"), axis=1, tiled=True),
        lax.all_gather(lowrank_up_factor, ("tp", "sub"), axis=1, tiled=True),
        lax.all_gather(magnitude, ("tp", "sub"), axis=0, tiled=True),
    )
    piece_count = piece_owner_blocks.shape[0]
    rollout_block_rows = down_all.shape[1] // piece_count
    blocks_own = local_rows // rollout_block_rows
    wanted = tp_index * blocks_own + jnp.arange(blocks_own)
    selector = (piece_owner_blocks[None, :] == wanted[:, None]).astype(jnp.bfloat16)
    down_local = (
        jnp.einsum(
            "jk,rkc->rjc",
            selector,
            down_all.reshape(UPDATE_RANK, piece_count, rollout_block_rows),
            preferred_element_type=jnp.float32,
        )
        .astype(jnp.bfloat16)
        .reshape(UPDATE_RANK, local_rows)
    )
    query_all = lax.all_gather(queries, "tp", axis=1, tiled=True).reshape(
        seq_count, KVH, group_size, HD
    )
    keys_local = key_value_cache[:, 0].reshape(seq_count, cache_len, KVH, HD)
    values_local = key_value_cache[:, 1].reshape(seq_count, cache_len, KVH, HD)
    positions = tp_index * cache_len + jnp.arange(cache_len)
    valid_mask = positions[None, :] < lengths[:, None]
    scores = (
        jnp.einsum("skgd,spkd->skgp", query_all, keys_local, preferred_element_type=jnp.float32)
        * score_scale
    )
    scores = jnp.where(valid_mask[:, None, None, :], scores, -1e30)
    peak_part = lax.pmax(jnp.max(scores, axis=-1), "tp")
    new_key = fresh_token_entries[:, 0].reshape(seq_count, KVH, HD)
    new_value = fresh_token_entries[:, 1].reshape(seq_count, KVH, HD).astype(jnp.float32)
    own_score = (
        jnp.einsum("skgd,skd->skg", query_all, new_key, preferred_element_type=jnp.float32)
        * score_scale
    )
    peak_all = jnp.maximum(peak_part, own_score)
    weights = jnp.where(valid_mask[:, None, None, :], jnp.exp(scores - peak_all[..., None]), 0.0)
    weighted = jnp.einsum(
        "skgp,spkd->skgd",
        weights.astype(jnp.bfloat16),
        values_local,
        preferred_element_type=jnp.float32,
    )
    weights_sum = jnp.sum(weights, axis=-1)
    combined = frozen_base_matrix.astype(jnp.float32) + expand_rank(down_local, up_all)
    square_part = jnp.sum(combined * combined, axis=0)
    own_weight = jnp.exp(own_score - peak_all)
    own_rounded = lax.optimization_barrier(own_weight.astype(jnp.bfloat16)).astype(jnp.float32)
    column_total = lax.psum(square_part, "tp")
    weighted_all, weights_all = lax.psum((weighted, weights_sum), "tp")
    numer = weighted_all + own_rounded[..., None] * new_value[:, :, None, :]
    denom = weights_all + own_weight
    context = (numer / denom[..., None]).reshape(seq_count, HEADS * HD).astype(jnp.bfloat16)
    context_local = lax.dynamic_slice_in_dim(context, tp_index * local_rows, local_rows, 1)
    column_norms = jnp.sqrt(column_total + norm_eps)
    merged_matrix = (combined * (magnitudes.astype(jnp.float32) / column_norms)).astype(
        jnp.bfloat16
    )
    partial_out = jnp.dot(context_local, merged_matrix, preferred_element_type=jnp.float32)
    return lax.psum_scatter(partial_out, "tp", scatter_dimension=1, tiled=True).astype(jnp.bfloat16)


def fused_kernel(
    sizes,
    lengths_ref,
    owner_ref,
    query_ref,
    fresh_ref,
    down_ref,
    up_ref,
    magnitude_ref,
    cache_ref,
    base_ref,
    out_ref,
    query_f32,
    query_all,
    cache,
    base,
    combined,
    pieces,
    down_local,
    up,
    magnitudes,
    part_send,
    part_recv,
    context_all,
    context_f32,
    norm_acc,
    norm_send,
    norm_recv,
    proj_send,
    proj_recv,
    cache_sem,
    base_sem,
    query_s,
    query_r,
    piece_s,
    piece_r,
    forward_s,
    forward_r,
    up_s,
    up_r,
    own_s,
    own_r,
    mag_s,
    mag_r,
    part_s,
    part_r,
    context_s,
    context_r,
    norm_s,
    norm_r,
    proj_s,
    proj_r,
):
    tp, dp, sub = sizes["tp"], sizes["dp"], sizes["sub"]
    owners = dp * sub
    t, d, s = lax.axis_index("tp"), lax.axis_index("dp"), lax.axis_index("sub")
    q = d + dp * s
    other = 1 - s
    seqs = query_ref.shape[0]
    heads = HEADS // tp
    half = heads // 2
    rows, columns = base.shape
    cache_len = cache.shape[2]
    score_scale = HD ** (-0.5)
    f32, bf16 = jnp.float32, jnp.bfloat16

    def place(tp_index, owner):
        return {"tp": tp_index, "dp": lax.rem(owner, dp), "sub": owner // dp}

    def peer_of(r):
        if r == 1:
            return t + 1 - 2 * lax.rem(t, 2)
        if r == 2:
            return t + 2 - 4 * (t // 2)
        return tp - 1 - t

    def remote(src, dst, send, recv, where):
        return pltpu.make_async_remote_copy(
            src_ref=src,
            dst_ref=dst,
            send_sem=send,
            recv_sem=recv,
            device_id=where,
            device_id_type=pl.DeviceIdType.MESH,
        )

    cache_copies = [
        pltpu.make_async_copy(cache_ref.at[:, i], cache.at[:, i], cache_sem.at[i]) for i in range(2)
    ]
    for copy in cache_copies:
        copy.start()
    base_copy = pltpu.make_async_copy(
        base_ref.at[:, pl.ds(pl.multiple_of(q * columns, columns), columns)], base, base_sem
    )
    base_copy.start()

    barrier = pltpu.get_barrier_semaphore()
    greeted = [place(peer_of(r), q) for r in range(1, tp)]
    greeted += [place(t, lax.rem(q + k, owners)) for k in range(1, owners)]
    for where in greeted:
        pl.semaphore_signal(
            barrier, inc=1, device_id=where, device_id_type=pl.DeviceIdType.MESH
        )

    for h in range(heads):
        query_f32[pl.ds(h, seqs, stride=heads), :] = query_ref[:, h * HD : (h + 1) * HD].astype(f32)
    own_query = query_f32[...].reshape(seqs, heads, HD)
    query_all[t] = own_query.astype(bf16)
    pieces[t * sub + s] = down_ref[...]
    magnitudes[s] = magnitude_ref[...].astype(f32).reshape(1, -1)

    row_index = lax.broadcasted_iota(jnp.int32, (heads, HD), 0)
    lane_index = lax.broadcasted_iota(jnp.int32, (heads, HD), 1)
    upper = row_index < half
    position = t * cache_len + lax.broadcasted_iota(jnp.int32, (heads, cache_len), 1)

    for copy in cache_copies:
        copy.wait()

    def split3(value):
        terms = []
        for _ in range(3):
            term = value.astype(bf16).astype(f32)
            terms.append(term)
            value = value - term
        return terms

    def joined(stats, first, i):
        lanes = [stats[:, (first + n) * seqs + i : (first + n) * seqs + i + 1] for n in range(3)]
        return (lanes[0] + lanes[1]) + lanes[2]

    def attend(tp_index):
        span = pl.ds(pl.multiple_of(tp_index * 2 * HD, 2 * HD), 2 * HD)
        stats = jnp.zeros((heads, HD), f32)
        for i in range(seqs):
            query = query_all[tp_index, i].astype(f32)
            left = jnp.where(upper, query, 0.0).astype(bf16)
            right = jnp.where(upper, 0.0, query).astype(bf16)
            scores = (
                lax.dot_general(
                    jnp.concatenate([left, right], axis=1),
                    cache[i, 0, :, span],
                    (((1,), (1,)), ((), ())),
                    preferred_element_type=f32,
                )
                * score_scale
            )
            valid = position < lengths_ref[i]
            scores = jnp.where(valid, scores, -1e30)
            peak = jnp.max(scores, axis=-1, keepdims=True)
            weights = jnp.where(valid, jnp.exp(scores - peak), 0.0)
            total = jnp.sum(weights, axis=-1, keepdims=True)
            both = jnp.dot(
                weights.astype(bf16), cache[i, 1, :, span], preferred_element_type=f32
            )
            part_send[tp_index, i] = jnp.where(upper, both[:, :HD], both[:, HD:]).astype(bf16)
            for term, value in enumerate(split3(peak) + split3(total)):
                stats = jnp.where(lane_index == term * seqs + i, value, stats)
        part_send[tp_index, seqs] = stats.astype(bf16)

    attend(t)
    part_recv[t] = part_send[t]

    pl.semaphore_wait(barrier, len(greeted))

    sibling = place(t, d + dp * other)
    mine = t * sub + s
    piece_columns = pieces.shape[2] // dp

    def part_of(piece, which_half):
        return pieces.at[
            piece, :, pl.ds(pl.multiple_of(which_half * piece_columns, piece_columns), piece_columns)
        ]

    query_copies, piece_copies = [], []
    for r in (3, 2, 1):
        copy = remote(
            query_all.at[t], query_all.at[t], query_s.at[r], query_r.at[t], place(peer_of(r), q)
        )
        copy.start()
        query_copies.append(copy)
    for r in (3, 2, 1):
        copy = remote(
            part_of(mine, d),
            part_of(mine, d),
            piece_s.at[r],
            piece_r.at[t],
            place(peer_of(r), q),
        )
        copy.start()
        piece_copies.append(copy)
    for src, send, recv in ((pieces.at[mine], own_s, own_r), (magnitudes.at[s], mag_s, mag_r)):
        copy = remote(src, src, send, recv, sibling)
        copy.start()
        piece_copies.append(copy)

    up_here = d == lax.rem(t, dp)
    up_owner = t // dp

    def up_copy(r):
        return remote(
            up_ref, up.at[s], up_s.at[r], up_r.at[s], place(peer_of(r) if r else t, t)
        )

    up_self = jnp.logical_and(up_here, s == up_owner)

    @pl.when(jnp.logical_and(up_here, s != up_owner))
    def _():
        up_copy(0).start()

    @pl.when(up_self)
    def _():
        up[s] = up_ref[...]

    part_copies = []
    for r in range(1, tp):
        peer = peer_of(r)
        remote(
            query_all.at[peer], query_all.at[peer], query_s.at[r], query_r.at[peer], place(peer, q)
        ).wait_recv()
        attend(peer)

        @pl.when(up_here)
        def _():
            up_copy(r).start()

        copy = remote(
            part_send.at[peer], part_recv.at[t], part_s.at[r], part_r.at[t], place(peer, q)
        )
        copy.start()
        part_copies.append(copy)

    forward_copies = []
    for r in range(1, tp):
        peer = peer_of(r)
        got = part_of(peer * sub + s, d)
        remote(got, got, piece_s.at[r], piece_r.at[peer], place(peer, q)).wait_recv()
        for k in range(1, owners):
            copy = remote(
                got,
                got,
                forward_s.at[r, k],
                forward_r.at[peer, q],
                place(t, lax.rem(q + k, owners)),
            )
            copy.start()
            forward_copies.append(copy)

    fresh = [
        [
            fresh_ref[
                i, :, pl.ds(pl.multiple_of((t * 2 + j) * HD, HD), HD)
            ].astype(f32)
            for j in range(2)
        ]
        for i in range(seqs)
    ]
    own_scores, own_values = [], []
    for i in range(seqs):
        key = jnp.where(upper, fresh[i][0][0:1], fresh[i][1][0:1])
        own_values.append(jnp.where(upper, fresh[i][0][1:2], fresh[i][1][1:2]))
        rows_of_query = query_f32[i * heads : (i + 1) * heads, :]
        own_scores.append(jnp.sum(rows_of_query * key, axis=-1, keepdims=True) * score_scale)

    for r in range(1, tp):
        peer = peer_of(r)
        remote(
            part_send.at[peer], part_recv.at[peer], part_s.at[r], part_r.at[peer], place(peer, q)
        ).wait_recv()

    all_stats = [part_recv[k, seqs].astype(f32) for k in range(tp)]
    for i in range(seqs):
        peaks = [joined(x, 0, i) for x in all_stats]
        peak = own_scores[i]
        for x in peaks:
            peak = jnp.maximum(peak, x)
        own_weight = jnp.exp(own_scores[i] - peak)
        numer = own_weight.astype(bf16).astype(f32) * own_values[i]
        denom = own_weight
        for k in range(tp):
            factor = jnp.exp(peaks[k] - peak)
            numer = numer + factor * part_recv[k, i].astype(f32)
            denom = denom + factor * joined(all_stats[k], 3, i)
        context_all[q, i] = (numer / denom).astype(bf16)

    context_copies = []
    for k in range(1, owners):
        copy = remote(
            context_all.at[q],
            context_all.at[q],
            context_s.at[k],
            context_r.at[q],
            place(t, lax.rem(q + k, owners)),
        )
        copy.start()
        context_copies.append(copy)
    for j in range(sub):

        @pl.when(jnp.logical_or(t != q, s != j))
        def _():
            remote(up_ref, up.at[j], up_s.at[0], up_r.at[j], place(t, q)).wait_recv()

    got = pieces.at[t * sub + other]
    remote(got, got, own_s, own_r, sibling).wait_recv()
    for r in range(1, tp):
        peer = peer_of(r)
        for k in range(1, owners):
            source = lax.rem(q + k, owners)
            got = part_of(peer * sub + source // dp, lax.rem(source, dp))
            remote(
                got, got, forward_s.at[r, k], forward_r.at[peer, source], place(t, source)
            ).wait_recv()

    piece_rows = pieces.shape[2]
    for j in range(rows // piece_rows):
        wanted = t * (rows // piece_rows) + j
        found = jnp.int32(0)
        for k in range(pieces.shape[0]):
            found = jnp.where(owner_ref[k] == wanted, k, found)
        down_local[:, j * piece_rows : (j + 1) * piece_rows] = pieces[found]

    base_copy.wait()
    norm_acc[...] = jnp.zeros_like(norm_acc)
    block = 256
    up_all = jnp.concatenate([up[j] for j in range(sub)], axis=1)

    def merge(c, carry):
        here = pl.ds(pl.multiple_of(c * block, block), block)
        down_rows = down_local[:, here]
        for n in range(columns // block):
            cols = slice(n * block, (n + 1) * block)
            tile = base[here, cols].astype(f32) + lax.dot_general(
                down_rows, up_all[:, cols], (((0,), (0,)), ((), ())), preferred_element_type=f32
            )
            norm_acc[:, cols] += jnp.sum((tile * tile).reshape(block // 8, 8, block), axis=0)
            combined[here, cols] = tile.astype(bf16)
        return carry

    lax.fori_loop(0, rows // block, merge, 0)
    norm_send[...] = jnp.sum(norm_acc[...], axis=0, keepdims=True)

    def result_copy(src, dst, send, recv, k):
        return remote(
            src, dst.at[t], send.at[k], recv.at[t], place(q, lax.rem(q + k, owners))
        )

    itself = t == q

    def norm_copy(k):
        return result_copy(norm_send, norm_recv, norm_s, norm_r, k)

    for k in range(1, owners):
        norm_copy(k).start()

    @pl.when(jnp.logical_not(itself))
    def _():
        norm_copy(0).start()

    @pl.when(itself)
    def _():
        norm_recv[t] = norm_send[...]

    for k in range(1, owners):
        peer = lax.rem(q + k, owners)
        remote(
            context_all.at[peer],
            context_all.at[peer],
            context_s.at[k],
            context_r.at[peer],
            place(t, peer),
        ).wait_recv()

    total_seqs = owners * seqs
    context_f32[...] = context_all[...].astype(f32).reshape(total_seqs * heads, HD)
    context = jnp.concatenate(
        [context_f32[pl.ds(h, total_seqs, stride=heads), :].astype(bf16) for h in range(heads)],
        axis=1,
    )
    middle = columns // 2
    for n in range(columns // block):
        partial = jnp.dot(
            context, combined[:, n * block : (n + 1) * block], preferred_element_type=f32
        )
        for piece in range(block // HD):
            start = n * block + piece * HD
            side, lane = start // middle, start % middle
            for k in range(owners):
                proj_send[k, side * seqs : (side + 1) * seqs, lane : lane + HD] = partial[
                    k * seqs : (k + 1) * seqs, piece * HD : (piece + 1) * HD
                ]

    def proj_copy(k):
        return result_copy(
            proj_send.at[lax.rem(q + k, owners)], proj_recv, proj_s, proj_r, k
        )

    for k in range(1, owners):
        proj_copy(k).start()

    @pl.when(jnp.logical_not(itself))
    def _():
        proj_copy(0).start()

    @pl.when(itself)
    def _():
        proj_recv[t] = proj_send[q]

    remote(
        magnitudes.at[other], magnitudes.at[other], mag_s, mag_r, sibling
    ).wait_recv()

    def arrived(src, dst, send, recv):
        for k in range(tp):

            @pl.when(jnp.logical_or(q != t, t != k))
            def _():
                remote(src, dst.at[k], send.at[0], recv.at[k], place(k, t)).wait_recv()

    arrived(norm_send, norm_recv, norm_s, norm_r)
    squares = norm_recv[0]
    for k in range(1, tp):
        squares = squares + norm_recv[k]
    norms = jnp.sqrt(squares + norm_eps)
    arrived(proj_send.at[0], proj_recv, proj_s, proj_r)
    total = proj_recv[0]
    for k in range(1, tp):
        total = total + proj_recv[k]
    for side in range(2):
        scale = magnitudes[side] / norms[:, side * middle : (side + 1) * middle]
        out_ref[:, side * middle : (side + 1) * middle] = (
            total[side * seqs : (side + 1) * seqs] * scale
        ).astype(bf16)

    for copy in query_copies + piece_copies + forward_copies + part_copies + context_copies:
        copy.wait_send()

    @pl.when(up_here)
    def _():
        for r in range(1, tp):
            up_copy(r).wait_send()

    @pl.when(jnp.logical_and(up_here, s != up_owner))
    def _():
        up_copy(0).wait_send()

    for k in range(1, owners):
        norm_copy(k).wait_send()
        proj_copy(k).wait_send()

    @pl.when(jnp.logical_not(itself))
    def _():
        norm_copy(0).wait_send()
        proj_copy(0).wait_send()


def fused_local(
    sizes,
    queries,
    key_value_cache,
    fresh_token_entries,
    lengths,
    frozen_base_matrix,
    lowrank_down_factor,
    lowrank_up_factor,
    magnitude,
    piece_owner_blocks,
):
    tp, dp, sub = sizes["tp"], sizes["dp"], sizes["sub"]
    owners = dp * sub
    seqs = queries.shape[0]
    heads = HEADS // tp
    rows, width = frozen_base_matrix.shape
    columns = width // owners
    trainers = tp * sub
    f32, bf16 = jnp.float32, jnp.bfloat16
    sem = pltpu.SemaphoreType.DMA
    vmem = pl.BlockSpec(memory_space=pltpu.VMEM)
    smem = pl.BlockSpec(memory_space=pltpu.SMEM)
    anywhere = pl.BlockSpec(memory_space=pl.ANY)
    return pl.pallas_call(
        functools.partial(fused_kernel, sizes),
        out_shape=jax.ShapeDtypeStruct((seqs, width // tp), bf16),
        in_specs=[smem, smem, vmem, vmem, vmem, vmem, vmem, anywhere, anywhere],
        out_specs=vmem,
        scratch_shapes=[
            pltpu.VMEM((seqs * heads, HD), f32),
            pltpu.VMEM((tp, seqs, heads, HD), bf16),
            pltpu.VMEM(key_value_cache.shape, bf16),
            pltpu.VMEM((rows, columns), bf16),
            pltpu.VMEM((rows, columns), bf16),
            pltpu.VMEM((trainers,) + lowrank_down_factor.shape, bf16),
            pltpu.VMEM((UPDATE_RANK, rows), bf16),
            pltpu.VMEM((sub,) + lowrank_up_factor.shape, bf16),
            pltpu.VMEM((sub, 1, magnitude.shape[0]), f32),
            pltpu.VMEM((tp, seqs + 1, heads, HD), bf16),
            pltpu.VMEM((tp, seqs + 1, heads, HD), bf16),
            pltpu.VMEM((owners, seqs, heads, HD), bf16),
            pltpu.VMEM((owners * seqs * heads, HD), f32),
            pltpu.VMEM((8, columns), f32),
            pltpu.VMEM((1, columns), f32),
            pltpu.VMEM((tp, 1, columns), f32),
            pltpu.VMEM((owners, 2 * seqs, columns // 2), f32),
            pltpu.VMEM((tp, 2 * seqs, columns // 2), f32),
            sem((2,)),
            sem,
            sem((tp,)),
            sem((tp,)),
            sem((tp,)),
            sem((tp,)),
            sem((tp, owners)),
            sem((tp, owners)),
            sem((tp,)),
            sem((sub,)),
            sem,
            sem,
            sem,
            sem,
            sem((tp,)),
            sem((tp,)),
            sem((owners,)),
            sem((owners,)),
            sem((owners,)),
            sem((tp,)),
            sem((owners,)),
            sem((tp,)),
        ],
        compiler_params=pltpu.CompilerParams(
            collective_id=0, has_side_effects=True, vmem_limit_bytes=56 * 1024 * 1024
        ),
    )(
        lengths,
        piece_owner_blocks,
        queries,
        fresh_token_entries,
        lowrank_down_factor,
        lowrank_up_factor,
        magnitude,
        key_value_cache,
        frozen_base_matrix,
    )


def solution(mesh):
    in_specs = (
        P(("groups", "dp", "sub"), "tp"),
        P(("groups", "dp", "sub"), None, "tp", None),
        P(("groups", "dp", "sub"), None, None),
        P(("groups", "dp", "sub")),
        P("tp", None),
        P("groups", ("tp", "sub")),
        P("groups", ("tp", "sub")),
        P(("groups", "tp", "sub")),
        P("groups"),
    )
    out_specs = P(("groups", "dp", "sub"), "tp")
    sizes = dict(mesh.shape)
    owners = sizes["dp"] * sizes["sub"]
    fits = sizes["tp"] == owners and 2 * sizes["tp"] == KVH and sizes["sub"] == 2
    body = functools.partial(fused_local, sizes) if fits else local
    return jax.shard_map(body, mesh=mesh, in_specs=in_specs, out_specs=out_specs, check_vma=False)
```

```python
import functools

import jax
import jax.numpy as jnp
from jax import lax
from jax.experimental import pallas as pl
from jax.experimental.pallas import tpu as pltpu
from jax.sharding import PartitionSpec as P

HEADS = 64
KVH = 8
HD = 128
UPDATE_RANK = 16


norm_eps = 1e-06


def expand_rank(down_cols, up_rows):
    return lax.dot_general(
        down_cols, up_rows, (((0,), (0,)), ((), ())), preferred_element_type=jnp.float32
    )


def local(
    queries,
    key_value_cache,
    fresh_token_entries,
    lengths,
    frozen_base_matrix,
    lowrank_down_factor,
    lowrank_up_factor,
    magnitude,
    piece_owner_blocks,
):
    local_rows = frozen_base_matrix.shape[0]
    seq_count = queries.shape[0]
    cache_len = key_value_cache.shape[2]
    group_size = HEADS // KVH
    score_scale = HD ** (-0.5)
    tp_index = lax.axis_index("tp")
    down_all, up_all, magnitudes = (
        lax.all_gather(lowrank_down_factor, ("tp", "sub"), axis=1, tiled=True),
        lax.all_gather(lowrank_up_factor, ("tp", "sub"), axis=1, tiled=True),
        lax.all_gather(magnitude, ("tp", "sub"), axis=0, tiled=True),
    )
    piece_count = piece_owner_blocks.shape[0]
    rollout_block_rows = down_all.shape[1] // piece_count
    blocks_own = local_rows // rollout_block_rows
    wanted = tp_index * blocks_own + jnp.arange(blocks_own)
    selector = (piece_owner_blocks[None, :] == wanted[:, None]).astype(jnp.bfloat16)
    down_local = (
        jnp.einsum(
            "jk,rkc->rjc",
            selector,
            down_all.reshape(UPDATE_RANK, piece_count, rollout_block_rows),
            preferred_element_type=jnp.float32,
        )
        .astype(jnp.bfloat16)
        .reshape(UPDATE_RANK, local_rows)
    )
    query_all = lax.all_gather(queries, "tp", axis=1, tiled=True).reshape(
        seq_count, KVH, group_size, HD
    )
    keys_local = key_value_cache[:, 0].reshape(seq_count, cache_len, KVH, HD)
    values_local = key_value_cache[:, 1].reshape(seq_count, cache_len, KVH, HD)
    positions = tp_index * cache_len + jnp.arange(cache_len)
    valid_mask = positions[None, :] < lengths[:, None]
    scores = (
        jnp.einsum("skgd,spkd->skgp", query_all, keys_local, preferred_element_type=jnp.float32)
        * score_scale
    )
    scores = jnp.where(valid_mask[:, None, None, :], scores, -1e30)
    peak_part = lax.pmax(jnp.max(scores, axis=-1), "tp")
    new_key = fresh_token_entries[:, 0].reshape(seq_count, KVH, HD)
    new_value = fresh_token_entries[:, 1].reshape(seq_count, KVH, HD).astype(jnp.float32)
    own_score = (
        jnp.einsum("skgd,skd->skg", query_all, new_key, preferred_element_type=jnp.float32)
        * score_scale
    )
    peak_all = jnp.maximum(peak_part, own_score)
    weights = jnp.where(valid_mask[:, None, None, :], jnp.exp(scores - peak_all[..., None]), 0.0)
    weighted = jnp.einsum(
        "skgp,spkd->skgd",
        weights.astype(jnp.bfloat16),
        values_local,
        preferred_element_type=jnp.float32,
    )
    weights_sum = jnp.sum(weights, axis=-1)
    combined = frozen_base_matrix.astype(jnp.float32) + expand_rank(down_local, up_all)
    square_part = jnp.sum(combined * combined, axis=0)
    own_weight = jnp.exp(own_score - peak_all)
    own_rounded = lax.optimization_barrier(own_weight.astype(jnp.bfloat16)).astype(jnp.float32)
    column_total = lax.psum(square_part, "tp")
    weighted_all, weights_all = lax.psum((weighted, weights_sum), "tp")
    numer = weighted_all + own_rounded[..., None] * new_value[:, :, None, :]
    denom = weights_all + own_weight
    context = (numer / denom[..., None]).reshape(seq_count, HEADS * HD).astype(jnp.bfloat16)
    context_local = lax.dynamic_slice_in_dim(context, tp_index * local_rows, local_rows, 1)
    column_norms = jnp.sqrt(column_total + norm_eps)
    merged_matrix = (combined * (magnitudes.astype(jnp.float32) / column_norms)).astype(
        jnp.bfloat16
    )
    partial_out = jnp.dot(context_local, merged_matrix, preferred_element_type=jnp.float32)
    return lax.psum_scatter(partial_out, "tp", scatter_dimension=1, tiled=True).astype(jnp.bfloat16)


def fused_kernel(
    sizes,
    lengths_ref,
    owner_ref,
    query_ref,
    fresh_ref,
    down_ref,
    up_ref,
    magnitude_ref,
    cache_ref,
    base_ref,
    out_ref,
    query_f32,
    query_all,
    cache,
    base,
    combined,
    pieces,
    down_local,
    up,
    magnitudes,
    part_send,
    part_recv,
    context_all,
    context_f32,
    norm_acc,
    norm_send,
    norm_recv,
    proj_f32,
    proj_send,
    proj_recv,
    cache_sem,
    base_sem,
    query_s,
    query_r,
    piece_s,
    piece_r,
    forward_s,
    forward_r,
    up_s,
    up_r,
    own_s,
    own_r,
    mag_s,
    mag_r,
    part_s,
    part_r,
    context_s,
    context_r,
    norm_s,
    norm_r,
    proj_s,
    proj_r,
):
    tp, dp, sub = sizes["tp"], sizes["dp"], sizes["sub"]
    owners = dp * sub
    t, d, s = lax.axis_index("tp"), lax.axis_index("dp"), lax.axis_index("sub")
    q = d + dp * s
    other = 1 - s
    seqs = query_ref.shape[0]
    heads = HEADS // tp
    half = heads // 2
    rows, columns = base.shape
    cache_len = cache.shape[2]
    score_scale = HD ** (-0.5)
    f32, bf16 = jnp.float32, jnp.bfloat16

    def place(tp_index, owner):
        return {"tp": tp_index, "dp": lax.rem(owner, dp), "sub": owner // dp}

    def peer_of(r):
        if r == 1:
            return t + 1 - 2 * lax.rem(t, 2)
        if r == 2:
            return t + 2 - 4 * (t // 2)
        return tp - 1 - t

    def remote(src, dst, send, recv, where):
        return pltpu.make_async_remote_copy(
            src_ref=src,
            dst_ref=dst,
            send_sem=send,
            recv_sem=recv,
            device_id=where,
            device_id_type=pl.DeviceIdType.MESH,
        )

    cache_copies = [
        pltpu.make_async_copy(cache_ref.at[:, i], cache.at[:, i], cache_sem.at[i]) for i in range(2)
    ]
    for copy in cache_copies:
        copy.start()
    base_copy = pltpu.make_async_copy(
        base_ref.at[:, pl.ds(pl.multiple_of(q * columns, columns), columns)], base, base_sem
    )
    base_copy.start()

    proj_f32[...] = jnp.zeros_like(proj_f32)
    barrier = pltpu.get_barrier_semaphore()
    greeted = [place(peer_of(r), q) for r in range(1, tp)]
    greeted += [place(t, lax.rem(q + k, owners)) for k in range(1, owners)]
    for where in greeted:
        pl.semaphore_signal(
            barrier, inc=1, device_id=where, device_id_type=pl.DeviceIdType.MESH
        )

    for h in range(heads):
        query_f32[pl.ds(h, seqs, stride=heads), :] = query_ref[:, h * HD : (h + 1) * HD].astype(f32)
    own_query = query_f32[...].reshape(seqs, heads, HD)
    query_all[t] = own_query.astype(bf16)
    pieces[t * sub + s] = down_ref[...]
    magnitudes[s] = magnitude_ref[...].astype(f32).reshape(1, -1)

    row_index = lax.broadcasted_iota(jnp.int32, (heads, HD), 0)
    lane_index = lax.broadcasted_iota(jnp.int32, (heads, HD), 1)
    upper = row_index < half
    position = t * cache_len + lax.broadcasted_iota(jnp.int32, (heads, cache_len), 1)

    for copy in cache_copies:
        copy.wait()

    def split3(value):
        terms = []
        for _ in range(3):
            term = value.astype(bf16).astype(f32)
            terms.append(term)
            value = value - term
        return terms

    def joined(stats, first, i):
        lanes = [stats[:, (first + n) * seqs + i : (first + n) * seqs + i + 1] for n in range(3)]
        return (lanes[0] + lanes[1]) + lanes[2]

    def attend(tp_index):
        span = pl.ds(pl.multiple_of(tp_index * 2 * HD, 2 * HD), 2 * HD)
        stats = jnp.zeros((heads, HD), f32)
        for i in range(seqs):
            query = query_all[tp_index, i].astype(f32)
            left = jnp.where(upper, query, 0.0).astype(bf16)
            right = jnp.where(upper, 0.0, query).astype(bf16)
            scores = (
                lax.dot_general(
                    jnp.concatenate([left, right], axis=1),
                    cache[i, 0, :, span],
                    (((1,), (1,)), ((), ())),
                    preferred_element_type=f32,
                )
                * score_scale
            )
            valid = position < lengths_ref[i]
            scores = jnp.where(valid, scores, -1e30)
            peak = jnp.max(scores, axis=-1, keepdims=True)
            weights = jnp.where(valid, jnp.exp(scores - peak), 0.0)
            total = jnp.sum(weights, axis=-1, keepdims=True)
            both = jnp.dot(
                weights.astype(bf16), cache[i, 1, :, span], preferred_element_type=f32
            )
            part_send[tp_index, i] = jnp.where(upper, both[:, :HD], both[:, HD:]).astype(bf16)
            for term, value in enumerate(split3(peak) + split3(total)):
                stats = jnp.where(lane_index == term * seqs + i, value, stats)
        part_send[tp_index, seqs] = stats.astype(bf16)

    attend(t)
    part_recv[t] = part_send[t]

    pl.semaphore_wait(barrier, len(greeted))

    sibling = place(t, d + dp * other)
    mine = t * sub + s
    piece_columns = pieces.shape[2] // dp

    def part_of(piece, which_half):
        return pieces.at[
            piece, :, pl.ds(pl.multiple_of(which_half * piece_columns, piece_columns), piece_columns)
        ]

    query_copies, piece_copies = [], []
    for r in (3, 2, 1):
        copy = remote(
            query_all.at[t], query_all.at[t], query_s.at[r], query_r.at[t], place(peer_of(r), q)
        )
        copy.start()
        query_copies.append(copy)
    for r in (3, 2, 1):
        copy = remote(
            part_of(mine, d),
            part_of(mine, d),
            piece_s.at[r],
            piece_r.at[t],
            place(peer_of(r), q),
        )
        copy.start()
        piece_copies.append(copy)
    for src, send, recv in ((pieces.at[mine], own_s, own_r), (magnitudes.at[s], mag_s, mag_r)):
        copy = remote(src, src, send, recv, sibling)
        copy.start()
        piece_copies.append(copy)

    up_here = d == lax.rem(t, dp)
    up_owner = t // dp

    def up_copy(r):
        return remote(
            up_ref, up.at[s], up_s.at[r], up_r.at[s], place(peer_of(r) if r else t, t)
        )

    up_self = jnp.logical_and(up_here, s == up_owner)

    @pl.when(jnp.logical_and(up_here, s != up_owner))
    def _():
        up_copy(0).start()

    @pl.when(up_self)
    def _():
        up[s] = up_ref[...]

    part_copies = []
    for r in range(1, tp):
        peer = peer_of(r)
        remote(
            query_all.at[peer], query_all.at[peer], query_s.at[r], query_r.at[peer], place(peer, q)
        ).wait_recv()
        attend(peer)

        @pl.when(up_here)
        def _():
            up_copy(r).start()

        copy = remote(
            part_send.at[peer], part_recv.at[t], part_s.at[r], part_r.at[t], place(peer, q)
        )
        copy.start()
        part_copies.append(copy)

    forward_copies = []
    for r in range(1, tp):
        peer = peer_of(r)
        got = part_of(peer * sub + s, d)
        remote(got, got, piece_s.at[r], piece_r.at[peer], place(peer, q)).wait_recv()
        for k in range(1, owners):
            copy = remote(
                got,
                got,
                forward_s.at[r, k],
                forward_r.at[peer, q],
                place(t, lax.rem(q + k, owners)),
            )
            copy.start()
            forward_copies.append(copy)

    fresh = [
        [
            fresh_ref[
                i, :, pl.ds(pl.multiple_of((t * 2 + j) * HD, HD), HD)
            ].astype(f32)
            for j in range(2)
        ]
        for i in range(seqs)
    ]
    own_scores, own_values = [], []
    for i in range(seqs):
        key = jnp.where(upper, fresh[i][0][0:1], fresh[i][1][0:1])
        own_values.append(jnp.where(upper, fresh[i][0][1:2], fresh[i][1][1:2]))
        rows_of_query = query_f32[i * heads : (i + 1) * heads, :]
        own_scores.append(jnp.sum(rows_of_query * key, axis=-1, keepdims=True) * score_scale)

    for r in range(1, tp):
        peer = peer_of(r)
        remote(
            part_send.at[peer], part_recv.at[peer], part_s.at[r], part_r.at[peer], place(peer, q)
        ).wait_recv()

    all_stats = [part_recv[k, seqs].astype(f32) for k in range(tp)]
    for i in range(seqs):
        peaks = [joined(x, 0, i) for x in all_stats]
        peak = own_scores[i]
        for x in peaks:
            peak = jnp.maximum(peak, x)
        own_weight = jnp.exp(own_scores[i] - peak)
        numer = own_weight.astype(bf16).astype(f32) * own_values[i]
        denom = own_weight
        for k in range(tp):
            factor = jnp.exp(peaks[k] - peak)
            numer = numer + factor * part_recv[k, i].astype(f32)
            denom = denom + factor * joined(all_stats[k], 3, i)
        context_all[q, i] = (numer / denom).astype(bf16)

    context_copies = []
    for k in range(1, owners):
        copy = remote(
            context_all.at[q],
            context_all.at[q],
            context_s.at[k],
            context_r.at[q],
            place(t, lax.rem(q + k, owners)),
        )
        copy.start()
        context_copies.append(copy)
    for j in range(sub):

        @pl.when(jnp.logical_or(t != q, s != j))
        def _():
            remote(up_ref, up.at[j], up_s.at[0], up_r.at[j], place(t, q)).wait_recv()

    got = pieces.at[t * sub + other]
    remote(got, got, own_s, own_r, sibling).wait_recv()
    for r in range(1, tp):
        peer = peer_of(r)
        for k in range(1, owners):
            source = lax.rem(q + k, owners)
            got = part_of(peer * sub + source // dp, lax.rem(source, dp))
            remote(
                got, got, forward_s.at[r, k], forward_r.at[peer, source], place(t, source)
            ).wait_recv()

    piece_rows = pieces.shape[2]
    for j in range(rows // piece_rows):
        wanted = t * (rows // piece_rows) + j
        found = jnp.int32(0)
        for k in range(pieces.shape[0]):
            found = jnp.where(owner_ref[k] == wanted, k, found)
        down_local[:, j * piece_rows : (j + 1) * piece_rows] = pieces[found]

    base_copy.wait()
    norm_acc[...] = jnp.zeros_like(norm_acc)
    block = 256
    up_all = jnp.concatenate([up[j] for j in range(sub)], axis=1)

    def merge(c, carry):
        here = pl.ds(pl.multiple_of(c * block, block), block)
        down_rows = down_local[:, here]
        for n in range(columns // block):
            cols = slice(n * block, (n + 1) * block)
            tile = base[here, cols].astype(f32) + lax.dot_general(
                down_rows, up_all[:, cols], (((0,), (0,)), ((), ())), preferred_element_type=f32
            )
            norm_acc[:, cols] += jnp.sum((tile * tile).reshape(block // 8, 8, block), axis=0)
            combined[here, cols] = tile.astype(bf16)
        return carry

    lax.fori_loop(0, rows // block, merge, 0)
    norm_send[...] = jnp.sum(norm_acc[...], axis=0, keepdims=True)

    def result_copy(src, dst, send, recv, k):
        return remote(
            src, dst.at[t], send.at[k], recv.at[t], place(q, lax.rem(q + k, owners))
        )

    itself = t == q

    def norm_copy(k):
        return result_copy(norm_send, norm_recv, norm_s, norm_r, k)

    for k in range(1, owners):
        norm_copy(k).start()

    @pl.when(jnp.logical_not(itself))
    def _():
        norm_copy(0).start()

    @pl.when(itself)
    def _():
        norm_recv[t] = norm_send[...]

    for k in range(1, owners):
        peer = lax.rem(q + k, owners)
        remote(
            context_all.at[peer],
            context_all.at[peer],
            context_s.at[k],
            context_r.at[peer],
            place(t, peer),
        ).wait_recv()

    total_seqs = owners * seqs
    context_f32[...] = context_all[...].astype(f32).reshape(total_seqs * heads, HD)
    context = jnp.concatenate(
        [context_f32[pl.ds(h, total_seqs, stride=heads), :].astype(bf16) for h in range(heads)],
        axis=1,
    )
    middle = columns // 2
    def proj_copy(side, k):
        return remote(
            proj_send.at[side, lax.rem(q + k, owners)],
            proj_recv.at[side, t],
            proj_s.at[side, k],
            proj_r.at[side, t],
            place(q, lax.rem(q + k, owners)),
        )

    def send_side(side):
        proj_send[side] = proj_f32[side].astype(proj_send.dtype)
        for k in range(1, owners):
            proj_copy(side, k).start()

        @pl.when(jnp.logical_not(itself))
        def _():
            proj_copy(side, 0).start()

        @pl.when(itself)
        def _():
            proj_recv[side, t] = proj_send[side, q]

    for n in range(columns // block):
        partial = jnp.dot(
            context, combined[:, n * block : (n + 1) * block], preferred_element_type=f32
        )
        for piece in range(block // HD):
            start = n * block + piece * HD
            side, lane = start // middle, start % middle
            for k in range(owners):
                proj_f32[side, k, lane // HD * seqs : (lane // HD + 1) * seqs, :] = partial[
                    k * seqs : (k + 1) * seqs, piece * HD : (piece + 1) * HD
                ]
        for side in range(2):
            if n * block < (side + 1) * middle <= (n + 1) * block:
                send_side(side)

    remote(
        magnitudes.at[other], magnitudes.at[other], mag_s, mag_r, sibling
    ).wait_recv()

    def arrived(src, dst, send, recv):
        for k in range(tp):

            @pl.when(jnp.logical_or(q != t, t != k))
            def _():
                remote(src, dst.at[k], send.at[0], recv.at[k], place(k, t)).wait_recv()

    arrived(norm_send, norm_recv, norm_s, norm_r)
    squares = norm_recv[0]
    for k in range(1, tp):
        squares = squares + norm_recv[k]
    norms = jnp.sqrt(squares + norm_eps)
    for side in range(2):
        arrived(proj_send.at[side, 0], proj_recv.at[side], proj_s.at[side], proj_r.at[side])
        total = proj_recv[side, 0].astype(f32)
        for k in range(1, tp):
            total = total + proj_recv[side, k].astype(f32)
        scale = magnitudes[side] / norms[:, side * middle : (side + 1) * middle]
        for n in range(middle // HD):
            lanes = slice(n * HD, (n + 1) * HD)
            out_ref[:, side * middle + n * HD : side * middle + (n + 1) * HD] = (
                total[n * seqs : (n + 1) * seqs] * scale[:, lanes]
            ).astype(bf16)

    for copy in query_copies + piece_copies + forward_copies + part_copies + context_copies:
        copy.wait_send()

    @pl.when(up_here)
    def _():
        for r in range(1, tp):
            up_copy(r).wait_send()

    @pl.when(jnp.logical_and(up_here, s != up_owner))
    def _():
        up_copy(0).wait_send()

    for k in range(1, owners):
        norm_copy(k).wait_send()
        for side in range(2):
            proj_copy(side, k).wait_send()

    @pl.when(jnp.logical_not(itself))
    def _():
        norm_copy(0).wait_send()
        for side in range(2):
            proj_copy(side, 0).wait_send()


def fused_local(
    sizes,
    queries,
    key_value_cache,
    fresh_token_entries,
    lengths,
    frozen_base_matrix,
    lowrank_down_factor,
    lowrank_up_factor,
    magnitude,
    piece_owner_blocks,
):
    tp, dp, sub = sizes["tp"], sizes["dp"], sizes["sub"]
    owners = dp * sub
    seqs = queries.shape[0]
    heads = HEADS // tp
    rows, width = frozen_base_matrix.shape
    columns = width // owners
    trainers = tp * sub
    sent_rows = -(-(columns // 2 // HD * seqs) // 16) * 16
    f32, bf16 = jnp.float32, jnp.bfloat16
    sem = pltpu.SemaphoreType.DMA
    vmem = pl.BlockSpec(memory_space=pltpu.VMEM)
    smem = pl.BlockSpec(memory_space=pltpu.SMEM)
    anywhere = pl.BlockSpec(memory_space=pl.ANY)
    return pl.pallas_call(
        functools.partial(fused_kernel, sizes),
        out_shape=jax.ShapeDtypeStruct((seqs, width // tp), bf16),
        in_specs=[smem, smem, vmem, vmem, vmem, vmem, vmem, anywhere, anywhere],
        out_specs=vmem,
        scratch_shapes=[
            pltpu.VMEM((seqs * heads, HD), f32),
            pltpu.VMEM((tp, seqs, heads, HD), bf16),
            pltpu.VMEM(key_value_cache.shape, bf16),
            pltpu.VMEM((rows, columns), bf16),
            pltpu.VMEM((rows, columns), bf16),
            pltpu.VMEM((trainers,) + lowrank_down_factor.shape, bf16),
            pltpu.VMEM((UPDATE_RANK, rows), bf16),
            pltpu.VMEM((sub,) + lowrank_up_factor.shape, bf16),
            pltpu.VMEM((sub, 1, magnitude.shape[0]), f32),
            pltpu.VMEM((tp, seqs + 1, heads, HD), bf16),
            pltpu.VMEM((tp, seqs + 1, heads, HD), bf16),
            pltpu.VMEM((owners, seqs, heads, HD), bf16),
            pltpu.VMEM((owners * seqs * heads, HD), f32),
            pltpu.VMEM((8, columns), f32),
            pltpu.VMEM((1, columns), f32),
            pltpu.VMEM((tp, 1, columns), f32),
            pltpu.VMEM((2, owners, sent_rows, HD), f32),
            pltpu.VMEM((2, owners, sent_rows, HD), bf16),
            pltpu.VMEM((2, tp, sent_rows, HD), bf16),
            sem((2,)),
            sem,
            sem((tp,)),
            sem((tp,)),
            sem((tp,)),
            sem((tp,)),
            sem((tp, owners)),
            sem((tp, owners)),
            sem((tp,)),
            sem((sub,)),
            sem,
            sem,
            sem,
            sem,
            sem((tp,)),
            sem((tp,)),
            sem((owners,)),
            sem((owners,)),
            sem((owners,)),
            sem((tp,)),
            sem((2, owners)),
            sem((2, tp)),
        ],
        compiler_params=pltpu.CompilerParams(
            collective_id=0, has_side_effects=True, vmem_limit_bytes=56 * 1024 * 1024
        ),
    )(
        lengths,
        piece_owner_blocks,
        queries,
        fresh_token_entries,
        lowrank_down_factor,
        lowrank_up_factor,
        magnitude,
        key_value_cache,
        frozen_base_matrix,
    )


def solution(mesh):
    in_specs = (
        P(("groups", "dp", "sub"), "tp"),
        P(("groups", "dp", "sub"), None, "tp", None),
        P(("groups", "dp", "sub"), None, None),
        P(("groups", "dp", "sub")),
        P("tp", None),
        P("groups", ("tp", "sub")),
        P("groups", ("tp", "sub")),
        P(("groups", "tp", "sub")),
        P("groups"),
    )
    out_specs = P(("groups", "dp", "sub"), "tp")
    sizes = dict(mesh.shape)
    owners = sizes["dp"] * sizes["sub"]
    fits = sizes["tp"] == owners and 2 * sizes["tp"] == KVH and sizes["sub"] == 2
    body = functools.partial(fused_local, sizes) if fits else local
    return jax.shard_map(body, mesh=mesh, in_specs=in_specs, out_specs=out_specs, check_vma=False)
```
